32 devices in a mesh: ctx: 32 (over z, y, x, core), head: 1.
Axes of the slice: x: 2, y: 2, z: 4, core: 2. Of those that a mesh axis runs over, the one named last changes fastest.
Arguments:
- queries: bfloat16 [6144, 4096], P('ctx', 'head'), may hold values from -96 to 96
- key_rows: bfloat16 [6144, 4096], P('ctx', 'head'), may hold values from -8 to 8
- value_rows: bfloat16 [6144, 4096], P('ctx', 'head'), may hold values from -6 to 6
- token_rates: float32 [6144, 8], P('ctx', 'head'), may hold values from 0.02 to 1
- fast_one: bfloat16 [8, 512, 512], P('head'), may hold values from -0.25 to 0.25
- fast_three: bfloat16 [8, 512, 512], P('head'), may hold values from -0.25 to 0.25
- fast_two: bfloat16 [8, 512, 512], P('head'), may hold values from -0.25 to 0.25
- head_gain: float32 [8], P('head'), may hold values from 0.5 to 1.5
Outputs:
- window_out: bfloat16 [6144, 4096], P('ctx', 'head')
- fast_out: bfloat16 [6144, 4096], P('ctx', 'head')
The draws below stay inside these ranges and needn't reach their ends.
All inputs are finite; a program needn't handle non-finite values.
Results may differ from the reference program's by a relative error of at most 0.011.
Values may be sent and summed in bfloat16 or wider, within the bound.
A program may use at most 128 MiB of HBM per device.

```python
import math
import jax
import jax.numpy as jnp
from jax import lax

HEADS = 8
HD = 512
FH = 512
TOK_DEV = 192
WINDOW = 1024
NS_STEPS = 2
TOKENS = 6144
N_CTX = 32


def drawn_pair(key):
    query_base = jnp.clip(jax.random.normal(jax.random.fold_in(key, 11), (TOKENS, HEADS * HD), jnp.float32), -6.0, 6.0)
    key_base = jnp.clip(jax.random.normal(jax.random.fold_in(key, 12), (TOKENS, HEADS * HD), jnp.float32), -6.0, 6.0)
    return (query_base, key_base)


def draw_queries(key, part):
    return drawn_pair(key)[0].astype(jnp.bfloat16)


def draw_key_rows(key, part):
    return drawn_pair(key)[1].astype(jnp.bfloat16)


def steps_of(stream_key, dims, pieces, smallest, top_value):
    def one(dim, blocks):
        steps = jax.random.uniform(jax.random.fold_in(jax.random.fold_in(stream_key, 6), dim), (blocks,), jnp.float32, smallest / len(pieces), top_value / len(pieces))
        return jnp.repeat(jnp.exp(steps), dims[dim] // blocks).reshape((-1,) + (1,) * (len(dims) - dim - 1))

    loudness = one(*pieces[0])
    for cut in pieces[1:]:
        loudness = loudness * one(*cut)
    return loudness


def noise(stream_key, dims, scale, limit, shards=(), kind=jnp.bfloat16):
    array = jax.random.normal(stream_key, dims, jnp.float32) * scale
    if len(shards) > 0:
        array = steps_of(stream_key, dims, shards, -0.22, 0.18) * array
    return jnp.clip(array, min=-limit, max=limit).astype(kind)


def setup_inputs(seed: int = 0) -> dict:
    streams_of = jax.random.split(jax.random.key(seed), 9)
    queries = draw_queries(jax.random.fold_in(streams_of[8], 71), 0)
    key_rows = draw_key_rows(jax.random.fold_in(streams_of[8], 71), 0)
    value_rows = noise(streams_of[2], (TOKENS, HEADS * HD), 1.0, 6.0, ((0, 32),))
    token_rates = jnp.clip(jnp.exp(math.log(1.0) - 3.912023 * jax.random.uniform(streams_of[3], (TOKENS, HEADS), jnp.float32) ** steps_of(streams_of[3], (TOKENS, HEADS), ((0, 32),), -0.2, 0.2)), 0.02, 1.0)
    fast_one = noise(streams_of[4], (HEADS, HD, FH), HD ** -0.5, 0.25)
    fast_three = noise(streams_of[5], (HEADS, HD, FH), HD ** -0.5, 0.25)
    fast_two = noise(streams_of[6], (HEADS, FH, HD), FH ** -0.5, 0.25)
    head_gain = jnp.clip(jnp.exp(jax.random.uniform(streams_of[7], (HEADS,), jnp.float32, math.log(0.5), math.log(1.5))), 0.5, 1.5)
    return {"queries": queries, "key_rows": key_rows, "value_rows": value_rows, "token_rates": token_rates, "fast_one": fast_one, "fast_three": fast_three, "fast_two": fast_two, "head_gain": head_gain}


COEF_A = 3.4445
COEF_B = -4.775
COEF_C = 2.0315
EPSILON = 1e-06

def rms_rows(block):
    return block / jnp.sqrt(lax.optimization_barrier(jnp.mean(block * block, axis=-1, keepdims=True)) + EPSILON)

def orthogonal(gradient):
    squares = jnp.sum(gradient * gradient)
    current = lax.optimization_barrier((gradient / (jnp.sqrt(squares) + 1e-07)).astype(jnp.bfloat16))
    for sweep_index in range(NS_STEPS):
        gram_matrix = lax.optimization_barrier(jnp.dot(current, current.T, preferred_element_type=jnp.float32).astype(jnp.bfloat16))
        mixer = (COEF_B * gram_matrix.astype(jnp.float32) + COEF_C * jnp.dot(gram_matrix, gram_matrix, preferred_element_type=jnp.float32)).astype(jnp.bfloat16)
        current = lax.optimization_barrier((COEF_A * current.astype(jnp.float32) + jnp.dot(mixer, current, preferred_element_type=jnp.float32)).astype(jnp.bfloat16))
    return current

def fast_head(operands):
    query_block, key_block, value_block, rate_column, weight_one, weight_three, weight_two = operands
    key_normed = rms_rows(key_block.astype(jnp.float32)).astype(jnp.bfloat16)
    query_normed = rms_rows(query_block.astype(jnp.float32)).astype(jnp.bfloat16)
    hidden_one = jnp.dot(key_normed, weight_one, preferred_element_type=jnp.float32)
    hidden_three = jnp.dot(key_normed, weight_three, preferred_element_type=jnp.float32)
    sigmoid_one = jax.nn.sigmoid(hidden_one)
    active = hidden_one * sigmoid_one
    hidden = (active * hidden_three).astype(jnp.bfloat16)
    delta_out = (-rate_column[:, None] * value_block.astype(jnp.float32)).astype(jnp.bfloat16)
    delta_hidden = jnp.dot(delta_out, weight_two.T, preferred_element_type=jnp.float32)
    delta_three = (delta_hidden * active).astype(jnp.bfloat16)
    delta_one = (delta_hidden * hidden_three * sigmoid_one * (1.0 + hidden_one * (1.0 - sigmoid_one))).astype(jnp.bfloat16)
    gradient_one = jnp.dot(key_normed.T, delta_one, preferred_element_type=jnp.float32)
    gradient_three = jnp.dot(key_normed.T, delta_three, preferred_element_type=jnp.float32)
    gradient_two = jnp.dot(hidden.T, delta_out, preferred_element_type=jnp.float32)
    new_one = (weight_one.astype(jnp.float32) - orthogonal(gradient_one).astype(jnp.float32)).astype(jnp.bfloat16)
    new_three = (weight_three.astype(jnp.float32) - orthogonal(gradient_three).astype(jnp.float32)).astype(jnp.bfloat16)
    new_two = (weight_two.astype(jnp.float32) - orthogonal(gradient_two).astype(jnp.float32)).astype(jnp.bfloat16)
    query_one = jnp.dot(query_normed, new_one, preferred_element_type=jnp.float32)
    query_three = jnp.dot(query_normed, new_three, preferred_element_type=jnp.float32)
    query_hidden = (jax.nn.silu(query_one) * query_three).astype(jnp.bfloat16)
    return jnp.dot(query_hidden, new_two, preferred_element_type=jnp.float32)

def window_head(operands):
    query_block, key_block, value_block = operands
    padded_keys = jnp.concatenate([jnp.zeros((WINDOW, HD), jnp.bfloat16), key_block], axis=0)
    padded_values = jnp.concatenate([jnp.zeros((WINDOW, HD), jnp.bfloat16), value_block], axis=0)

    def one_block(block_index):
        start = (block_index * TOK_DEV).astype(jnp.int32)
        queries_here = lax.dynamic_slice_in_dim(query_block, start, TOK_DEV, 0)
        keys_here = lax.dynamic_slice_in_dim(padded_keys, start, TOK_DEV + WINDOW, 0)
        values_here = lax.dynamic_slice_in_dim(padded_values, start, TOK_DEV + WINDOW, 0)
        scores = jnp.dot(queries_here, keys_here.T, preferred_element_type=jnp.float32) * HD ** (-0.5)
        query_pos = lax.broadcasted_iota(jnp.int32, (TOK_DEV, TOK_DEV + WINDOW), 0) + WINDOW
        key_pos = lax.broadcasted_iota(jnp.int32, (TOK_DEV, TOK_DEV + WINDOW), 1)
        offset = query_pos - key_pos
        allowed = (offset >= 0) & (offset < WINDOW) & (key_pos + start - WINDOW >= 0)
        scores = jnp.where(allowed, scores, -1e+30)
        row_top = lax.optimization_barrier(jnp.max(scores, axis=-1, keepdims=True))
        exponent = jnp.exp(scores - row_top)
        weights = (exponent / lax.optimization_barrier(jnp.sum(exponent, axis=-1, keepdims=True))).astype(jnp.bfloat16)
        return jnp.dot(weights, values_here, preferred_element_type=jnp.float32)
    blocks = lax.map(one_block, jnp.arange(N_CTX, dtype=jnp.int32))
    return blocks.reshape(TOKENS, HD)

def reference(queries, key_rows, value_rows, token_rates, fast_one, fast_three, fast_two, head_gain):
    split_q = queries.reshape(TOKENS, HEADS, HD).transpose(1, 0, 2)
    split_k = key_rows.reshape(TOKENS, HEADS, HD).transpose(1, 0, 2)
    split_v = value_rows.reshape(TOKENS, HEADS, HD).transpose(1, 0, 2)
    attended = lax.map(window_head, (split_q, split_k, split_v)).transpose(1, 0, 2)
    fast = lax.map(fast_head, (split_q, split_k, split_v, token_rates.T, fast_one, fast_three, fast_two))
    fast = (fast * head_gain[:, None, None]).transpose(1, 0, 2)
    window_out = attended / jnp.sqrt(lax.optimization_barrier(jnp.mean(attended * attended, axis=(1, 2), keepdims=True)) + EPSILON)
    fast_out = fast / jnp.sqrt(lax.optimization_barrier(jnp.mean(fast * fast, axis=(1, 2), keepdims=True)) + EPSILON)
    return (window_out.reshape(TOKENS, HEADS * HD).astype(jnp.bfloat16), fast_out.reshape(TOKENS, HEADS * HD).astype(jnp.bfloat16))
```

```python
import functools

import jax
import jax.numpy as jnp
from jax import lax
from jax.experimental import pallas as pl
from jax.experimental.pallas import tpu as pltpu
from jax.sharding import Mesh
from jax.sharding import PartitionSpec as P

WINDOW = 1024
NS_STEPS = 2

COEF_A = 3.4445
COEF_B = -4.775
COEF_C = 2.0315
EPSILON = 1e-06


def rms_heads(block):
    return block / jnp.sqrt(jnp.mean(block * block, axis=-1, keepdims=True) + EPSILON)


def to_heads(rows):
    return lax.all_to_all(rows, "mem", split_axis=1, concat_axis=0, tiled=True)


def to_tokens(rows):
    return lax.all_to_all(rows, "mem", split_axis=0, concat_axis=1, tiled=True)


def with_earlier(rows):
    tokens, groups = rows.shape[0], lax.axis_size("grp")
    parts, missing, distance = [rows], WINDOW, 1
    while missing > 0:
        take = min(missing, tokens)
        pairs = [(i, i + distance) for i in range(groups - distance)]
        parts.insert(0, lax.ppermute(rows[tokens - take :], "grp", pairs))
        missing -= take
        distance += 1
    return jnp.concatenate(parts, axis=0)


def window_attention(q, k, v):
    tokens, width = q.shape
    block = 512 if tokens % 512 == 0 else tokens
    count = tokens // block
    keys, values = with_earlier(k), with_earlier(v)
    reach = WINDOW + block
    keys = jnp.stack([keys[i * block : i * block + reach] for i in range(count)])
    values = jnp.stack([values[i * block : i * block + reach] for i in range(count)])
    scores = jnp.einsum(
        "bqd,bkd->bqk", q.reshape(count, block, width), keys, preferred_element_type=jnp.float32
    ) * width ** (-0.5)
    query_pos = lax.broadcasted_iota(jnp.int32, (count, block, reach), 1) + WINDOW
    key_pos = lax.broadcasted_iota(jnp.int32, (count, block, reach), 2)
    base = lax.broadcasted_iota(jnp.int32, (count, block, reach), 0) * block
    first_key = lax.axis_index("grp") * tokens - WINDOW
    offset = query_pos - key_pos
    allowed = (offset >= 0) & (offset < WINDOW) & (key_pos + base + first_key >= 0)
    scores = jnp.where(allowed, scores, -1e30)
    row_top = jnp.max(scores, axis=-1, keepdims=True)
    exponent = jnp.exp(scores - row_top)
    weights = (exponent / jnp.sum(exponent, axis=-1, keepdims=True)).astype(jnp.bfloat16)
    out = jnp.einsum("bqk,bkd->bqd", weights, values, preferred_element_type=jnp.float32)
    return out.reshape(tokens, width)


def orthogonal(gradient):
    squares = jnp.sum(gradient * gradient)
    current = (gradient / (jnp.sqrt(squares) + 1e-07)).astype(jnp.bfloat16)
    for sweep_index in range(NS_STEPS):
        gram = jnp.einsum(
            "rc,sc->rs", current, current, preferred_element_type=jnp.float32
        ).astype(jnp.bfloat16)
        mixer = (
            COEF_B * gram.astype(jnp.float32)
            + COEF_C * jnp.dot(gram, gram, preferred_element_type=jnp.float32)
        ).astype(jnp.bfloat16)
        current = (
            COEF_A * current.astype(jnp.float32)
            + jnp.dot(mixer, current, preferred_element_type=jnp.float32)
        ).astype(jnp.bfloat16)
    return current


def fast_weights(q, k, v, rates, one, three, two):
    f32 = jnp.float32
    key_normed = rms_heads(k.astype(f32)).astype(jnp.bfloat16)
    query_normed = rms_heads(q.astype(f32)).astype(jnp.bfloat16)
    hidden_one = jnp.dot(key_normed, one, preferred_element_type=f32)
    hidden_three = jnp.dot(key_normed, three, preferred_element_type=f32)
    sigmoid_one = jax.nn.sigmoid(hidden_one)
    active = hidden_one * sigmoid_one
    hidden = (active * hidden_three).astype(jnp.bfloat16)
    delta_out = (-rates * v.astype(f32)).astype(jnp.bfloat16)
    delta_hidden = jnp.einsum("td,fd->tf", delta_out, two, preferred_element_type=f32)
    delta_three = (delta_hidden * active).astype(jnp.bfloat16)
    delta_one = (
        delta_hidden * hidden_three * sigmoid_one * (1.0 + hidden_one * (1.0 - sigmoid_one))
    ).astype(jnp.bfloat16)
    gradient_one = jnp.einsum("td,tf->df", key_normed, delta_one, preferred_element_type=f32)
    gradient_three = jnp.einsum("td,tf->df", key_normed, delta_three, preferred_element_type=f32)
    gradient_two = jnp.einsum("tf,td->fd", hidden, delta_out, preferred_element_type=f32)
    grads = lax.psum(jnp.stack([gradient_one, gradient_three, gradient_two]), "grp")
    new = [
        (old.astype(f32) - orthogonal(grads[i]).astype(f32)).astype(jnp.bfloat16)
        for i, old in enumerate((one, three, two))
    ]
    query_one = jnp.dot(query_normed, new[0], preferred_element_type=f32)
    query_three = jnp.dot(query_normed, new[1], preferred_element_type=f32)
    query_hidden = (jax.nn.silu(query_one) * query_three).astype(jnp.bfloat16)
    return jnp.dot(query_hidden, new[2], preferred_element_type=f32)


def normed(rows):
    rows = rows.astype(jnp.float32)
    heads = lax.axis_size("head")
    total = lax.psum(jnp.sum(rows * rows, axis=1, keepdims=True), "head")
    return (rows / jnp.sqrt(total / (rows.shape[1] * heads) + EPSILON)).astype(jnp.bfloat16)


def local(queries, key_rows, value_rows, token_rates, fast_one, fast_three, fast_two, head_gain):
    me = lax.axis_index("mem")
    k, v, q = to_heads(key_rows), to_heads(value_rows), to_heads(queries)
    first = lax.axis_index("head") * head_gain.shape[0] if token_rates.shape[1] != head_gain.shape[0] else 0
    rates = lax.all_gather(token_rates, "mem", axis=0, tiled=True)
    rates = lax.dynamic_slice_in_dim(rates, me + first, 1, axis=1)
    one, three, two = (
        lax.dynamic_index_in_dim(w, me, 0, keepdims=False) for w in (fast_one, fast_three, fast_two)
    )
    gain = lax.dynamic_index_in_dim(head_gain, me, 0, keepdims=False)
    attended = window_attention(q, k, v)
    fast = fast_weights(q, k, v, rates, one, three, two) * gain
    window_rows = to_tokens(attended.astype(jnp.bfloat16))
    fast_rows = to_tokens(fast.astype(jnp.bfloat16))
    return normed(window_rows), normed(fast_rows)


def dot_nn(a, b):
    return jnp.dot(a, b, preferred_element_type=jnp.float32)


def dot_nt(a, b):
    return lax.dot_general(a, b, (((1,), (1,)), ((), ())), preferred_element_type=jnp.float32)


def dot_tn(a, b):
    return lax.dot_general(a, b, (((0,), (0,)), ((), ())), preferred_element_type=jnp.float32)


def layer_kernel(
    dims, k_hbm, v_hbm, q_hbm, rates_hbm, one_hbm, three_hbm, two_hbm, gain_ref,
    window_ref, fast_ref,
    kbuf, vbuf, qbuf, rbuf, weights, updated, grads, from_outer, from_inner, to_inner, to_outer,
    window_send, fast_send, window_recv, fast_recv,
    k_s, k_r, v_s, v_r, q_s, q_r, r_s, r_r, halo_s, halo_r, outer_r, inner_r, inner_s, outer_s,
    win_s, win_r, fast_s, fast_r, load_sem,
):
    groups, members, rows, width, pad, chunk = dims
    f32, bf16 = jnp.float32, jnp.bfloat16
    me, grp = lax.axis_index("mem"), lax.axis_index("grp")
    base = pad + WINDOW
    reach = base + rows
    stretch = members * rows
    chunks = 3 * width // chunk
    halo_first = (stretch - WINDOW) // rows
    halo_part = (halo_first + 1) * rows - (stretch - WINDOW)
    has_lower, has_upper = grp > 0, grp < groups - 1
    has_outer = jnp.logical_and(has_lower, has_upper)
    in_lower = grp < groups // 2
    inner = jnp.where(in_lower, grp + 1, grp - 1)
    outer = jnp.where(in_lower, grp - 1, grp + 1)
    is_mid = jnp.logical_or(grp == groups // 2 - 1, grp == groups // 2)

    barrier = pltpu.get_barrier_semaphore()
    for d in range(1, members):
        pl.semaphore_signal(barrier, inc=1, device_id={"mem": lax.rem(me + d, members)})

    @pl.when(has_lower)
    def _():
        pl.semaphore_signal(barrier, inc=1, device_id={"grp": grp - 1})

    @pl.when(has_upper)
    def _():
        pl.semaphore_signal(barrier, inc=1, device_id={"grp": grp + 1})

    pl.semaphore_wait(
        barrier, members - 1 + jnp.minimum(grp, 1) + jnp.minimum(groups - 1 - grp, 1)
    )

    def cols(p):
        return pl.ds(pl.multiple_of(p * width, width), width)

    def own_rows(s, first=base):
        return pl.ds(pl.multiple_of(first + s * rows, 16), rows)

    def exchange(hbm, buf, first, send, recv, d):
        peer = lax.rem(me + d, members)
        return pltpu.make_async_remote_copy(
            src_ref=hbm.at[:, cols(peer)], dst_ref=buf.at[own_rows(me, first)],
            send_sem=send.at[d], recv_sem=recv.at[d], device_id={"mem": peer},
        )

    def kept(hbm, buf, first, recv):
        return pltpu.make_async_copy(
            hbm.at[:, cols(me)], buf.at[own_rows(me, first)], recv.at[0]
        )

    def rates_to(d):
        peer = lax.rem(me + d, members)
        return pltpu.make_async_remote_copy(
            src_ref=rates_hbm.at[peer], dst_ref=rbuf.at[me],
            send_sem=r_s.at[d], recv_sem=r_r.at[d], device_id={"mem": peer},
        )

    def block_to(send_buf, recv_buf, send, recv, s):
        d = lax.rem(s - me + members, members)
        return pltpu.make_async_remote_copy(
            src_ref=send_buf.at[s], dst_ref=recv_buf.at[me],
            send_sem=send.at[d], recv_sem=recv.at[d], device_id={"mem": s},
        )

    own_rates = pltpu.make_async_copy(rates_hbm.at[me], rbuf.at[me], r_r.at[0])
    own_rates.start()
    kept(k_hbm, kbuf, base, k_r).start()
    kept(v_hbm, vbuf, base, v_r).start()
    kept(q_hbm, qbuf, 0, q_r).start()

    @pl.loop(1, members)
    def _(d):
        rates_to(d).start()
        exchange(k_hbm, kbuf, base, k_s, k_r, d).start()
        exchange(v_hbm, vbuf, base, v_s, v_r, d).start()

    loads = [
        pltpu.make_async_copy(hbm.at[me], weights.at[i], load_sem.at[i])
        for i, hbm in enumerate((one_hbm, three_hbm, two_hbm))
    ]
    for load in loads:
        load.start()
    kbuf[0:pad] = jnp.zeros((pad, width), bf16)
    vbuf[0:pad] = jnp.zeros((pad, width), bf16)

    @pl.when(grp == 0)
    def _():
        kbuf[pad:base] = jnp.zeros((WINDOW, width), bf16)
        vbuf[pad:base] = jnp.zeros((WINDOW, width), bf16)

    grads[...] = jnp.zeros_like(grads)
    for load in loads:
        load.wait()

    def halo_copies(s, size):
        start = base + s * rows + rows - size
        return [
            pltpu.make_async_remote_copy(
                src_ref=buf.at[pl.ds(pl.multiple_of(start, 16), size)],
                dst_ref=buf.at[pl.ds(pl.multiple_of(start - stretch, 16), size)],
                send_sem=halo_s.at[i, s], recv_sem=halo_r.at[i, s], device_id={"grp": grp + 1},
            )
            for i, buf in enumerate((kbuf, vbuf))
        ]

    def for_halo(s, present, act):
        @pl.when(jnp.logical_and(present, s == halo_first))
        def _():
            for copy in halo_copies(s, halo_part):
                act(copy)

        @pl.when(jnp.logical_and(present, s > halo_first))
        def _():
            for copy in halo_copies(s, rows):
                act(copy)

    def rms_unit(x):
        x = x.astype(f32)
        return (x * lax.rsqrt(jnp.mean(x * x, axis=1, keepdims=True) + EPSILON)).astype(bf16)

    @pl.loop(0, members)
    def _(d):
        s = lax.rem(me - d + members, members)

        @pl.when(d == 0)
        def _():
            own_rates.wait()
            kept(k_hbm, kbuf, base, k_r).wait()
            kept(v_hbm, vbuf, base, v_r).wait()

        @pl.when(d > 0)
        def _():
            rates_to(d).wait_recv()
            exchange(k_hbm, kbuf, base, k_s, k_r, d).wait_recv()
            exchange(v_hbm, vbuf, base, v_s, v_r, d).wait_recv()

        for_halo(s, has_upper, lambda copy: copy.start())

        @pl.when(d == members // 2)
        def _():
            @pl.loop(1, members)
            def _(e):
                exchange(q_hbm, qbuf, 0, q_s, q_r, e).start()

        key_unit = rms_unit(kbuf[own_rows(s)])
        rate_row = rbuf[s][0:1]
        lanes = rate_row.shape[1]
        diagonal = lax.broadcasted_iota(jnp.int32, (rows, lanes), 0) == lax.broadcasted_iota(
            jnp.int32, (rows, lanes), 1
        )
        rate = jnp.sum(jnp.where(diagonal, rate_row, 0.0), axis=1, keepdims=True)
        delta_out = (-rate * vbuf[own_rows(s)].astype(f32)).astype(bf16)
        a = dot_nn(key_unit, weights[0])
        b = dot_nn(key_unit, weights[1])
        dh = dot_nt(delta_out, weights[2])
        sig = 1.0 / (1.0 + jnp.exp(-a))
        active = a * sig
        hidden = (active * b).astype(bf16)
        delta_three = (dh * active).astype(bf16)
        delta_one = (dh * b * sig * (1.0 + a * (1.0 - sig))).astype(bf16)
        grads[0:width] += dot_tn(key_unit, delta_one)
        grads[width : 2 * width] += dot_tn(key_unit, delta_three)
        grads[2 * width : 3 * width] += dot_tn(hidden, delta_out)

    def rows_of(i):
        return pl.ds(pl.multiple_of(i * chunk, chunk), chunk)

    def inward(i, target, recv):
        return pltpu.make_async_remote_copy(
            src_ref=to_inner.at[i], dst_ref=target.at[i],
            send_sem=inner_s.at[i], recv_sem=recv.at[i], device_id={"grp": inner},
        )

    def outward(i):
        return pltpu.make_async_remote_copy(
            src_ref=to_outer.at[i], dst_ref=from_inner.at[i],
            send_sem=outer_s.at[i], recv_sem=inner_r.at[i], device_id={"grp": outer},
        )

    def send_inward(i):
        @pl.when(is_mid)
        def _():
            inward(i, from_inner, inner_r).start()

        @pl.when(jnp.logical_not(is_mid))
        def _():
            inward(i, from_outer, outer_r).start()

    @pl.when(jnp.logical_not(has_outer))
    def _():
        @pl.loop(0, chunks)
        def _(i):
            to_inner[i] = grads[rows_of(i)].astype(bf16)
            send_inward(i)

    def attend(s):
        scores = dot_nt(qbuf[own_rows(s, 0)], kbuf[pl.ds(pl.multiple_of(s * rows, 16), reach)])
        scores = scores * width ** (-0.5)
        query = lax.broadcasted_iota(jnp.int32, (rows, reach), 0)
        key = lax.broadcasted_iota(jnp.int32, (rows, reach), 1)
        offset = query - key + base
        first = grp * stretch + s * rows - base
        allowed = (offset >= 0) & (offset < WINDOW) & (key + first >= 0)
        scores = jnp.where(allowed, scores, -1e30)
        top = jnp.max(scores, axis=1, keepdims=True)
        exponent = jnp.exp(scores - top)
        total = jnp.sum(exponent, axis=1, keepdims=True)
        out = dot_nn(
            exponent.astype(bf16), vbuf[pl.ds(pl.multiple_of(s * rows, 16), reach)]
        )
        return (out / total).astype(bf16)

    lag = 2

    @pl.loop(0, chunks + lag)
    def _(i):
        @pl.when(jnp.logical_and(has_outer, i < chunks))
        def _():
            inward(i, from_outer, outer_r).wait_recv()
            partial = grads[rows_of(i)] + from_outer[i].astype(f32)
            to_inner[i] = partial.astype(bf16)
            send_inward(i)

        @pl.when(i >= lag)
        def _():
            j = i - lag
            outward(j).wait_recv()

            @pl.when(is_mid)
            def _():
                grads[rows_of(j)] = to_inner[j].astype(f32) + from_inner[j].astype(f32)

            @pl.when(jnp.logical_not(is_mid))
            def _():
                grads[rows_of(j)] = from_inner[j].astype(f32)

            @pl.when(has_outer)
            def _():
                to_outer[j] = grads[rows_of(j)].astype(bf16)
                outward(j).start()

        @pl.when(jnp.logical_and(i >= chunks - members, i < chunks))
        def _():
            s = chunks - 1 - i
            d = lax.rem(me - s + members, members)

            @pl.when(d == 0)
            def _():
                kept(q_hbm, qbuf, 0, q_r).wait()

            @pl.when(d > 0)
            def _():
                exchange(q_hbm, qbuf, 0, q_s, q_r, d).wait_recv()

            piece = s + halo_first
            for_halo(
                piece, jnp.logical_and(has_lower, piece < members), lambda copy: copy.wait_recv()
            )
            block = attend(s)

            @pl.when(s == me)
            def _():
                window_recv[s] = block

            @pl.when(s != me)
            def _():
                window_send[s] = block
                block_to(window_send, window_recv, win_s, win_r, s).start()

    @pl.loop(0, 3)
    def _(m):
        gradient = grads[pl.ds(pl.multiple_of(m * width, width), width)]
        squares = jnp.sum(jnp.sum(gradient * gradient, axis=1, keepdims=True), axis=0, keepdims=True)
        current = (gradient / (jnp.sqrt(squares) + 1e-07)).astype(bf16)
        for sweep_index in range(NS_STEPS):
            gram = dot_nt(current, current).astype(bf16)
            mixer = (COEF_B * gram.astype(f32) + COEF_C * dot_nn(gram, gram)).astype(bf16)
            current = (COEF_A * current.astype(f32) + dot_nn(mixer, current)).astype(bf16)
        updated[m] = (weights[m].astype(f32) - current.astype(f32)).astype(bf16)

    gain = gain_ref[me]

    @pl.loop(1, members + 1)
    def _(d):
        s = lax.rem(me + d, members)
        unit = rms_unit(qbuf[own_rows(s, 0)])
        a = dot_nn(unit, updated[0])
        b = dot_nn(unit, updated[1])
        hidden = (a / (1.0 + jnp.exp(-a)) * b).astype(bf16)
        block = (dot_nn(hidden, updated[2]) * gain).astype(bf16)

        @pl.when(s == me)
        def _():
            fast_recv[s] = block

        @pl.when(s != me)
        def _():
            fast_send[s] = block
            block_to(fast_send, fast_recv, fast_s, fast_r, s).start()

    def finish(recv, out):
        total = jnp.zeros((rows, 1), f32)
        for h in range(members):
            x = recv[h].astype(f32)
            total = total + jnp.sum(x * x, axis=1, keepdims=True)
        scale = lax.rsqrt(total / (members * width) + EPSILON)
        for h in range(members):
            out[:, h * width : (h + 1) * width] = (recv[h].astype(f32) * scale).astype(bf16)

    def arrivals(send_buf, recv_buf, send, recv):
        @pl.loop(1, members)
        def _(d):
            block_to(send_buf, recv_buf, send, recv, lax.rem(me + d, members)).wait_recv()

    arrivals(window_send, window_recv, win_s, win_r)
    finish(window_recv, window_ref)
    arrivals(fast_send, fast_recv, fast_s, fast_r)
    finish(fast_recv, fast_ref)

    @pl.loop(1, members)
    def _(d):
        s = lax.rem(me + d, members)
        rates_to(d).wait_send()
        exchange(k_hbm, kbuf, base, k_s, k_r, d).wait_send()
        exchange(v_hbm, vbuf, base, v_s, v_r, d).wait_send()
        exchange(q_hbm, qbuf, 0, q_s, q_r, d).wait_send()
        block_to(window_send, window_recv, win_s, win_r, s).wait_send()
        block_to(fast_send, fast_recv, fast_s, fast_r, s).wait_send()

    @pl.loop(0, members)
    def _(s):
        for_halo(s, has_upper, lambda copy: copy.wait_send())

    @pl.loop(0, chunks)
    def _(i):
        inward(i, from_inner, inner_r).wait_send()

        @pl.when(has_outer)
        def _():
            outward(i).wait_send()


def local_kernel(queries, key_rows, value_rows, token_rates, fast_one, fast_three, fast_two, head_gain):
    groups, members = lax.axis_size("grp"), lax.axis_size("mem")
    rows, width = queries.shape[0], fast_one.shape[1]
    pad = -(WINDOW + rows) % 128
    chunk = 128
    chunks = 3 * width // chunk
    lanes = rows + -rows % 128
    rates = jnp.pad(token_rates.T, ((0, 0), (0, lanes - rows)))
    rates = jnp.broadcast_to(rates[:, None, :], (members, 8, lanes))
    bf16, dma = jnp.bfloat16, pltpu.SemaphoreType.DMA
    keys = pltpu.VMEM((pad + WINDOW + members * rows, width), bf16)
    parts = pltpu.VMEM((chunks, chunk, width), bf16)
    blocks = pltpu.VMEM((members, rows, width), bf16)
    matrices = pltpu.VMEM((3, width, width), bf16)
    anywhere, vmem = pl.BlockSpec(memory_space=pl.ANY), pl.BlockSpec(memory_space=pltpu.VMEM)
    out = jax.ShapeDtypeStruct(queries.shape, bf16)
    return pl.pallas_call(
        functools.partial(layer_kernel, (groups, members, rows, width, pad, chunk)),
        out_shape=(out, out),
        in_specs=[anywhere] * 7 + [pl.BlockSpec(memory_space=pltpu.SMEM)],
        out_specs=(vmem, vmem),
        scratch_shapes=[
            keys, keys, pltpu.VMEM((members * rows, width), bf16),
            pltpu.VMEM((members, 8, lanes), jnp.float32),
            matrices, matrices, pltpu.VMEM((3 * width, width), jnp.float32),
            parts, parts, parts, parts, blocks, blocks, blocks, blocks,
        ]
        + [dma((members,))] * 8
        + [dma((2, members))] * 2
        + [dma((chunks,))] * 4
        + [dma((members,))] * 4
        + [dma((3,))],
        compiler_params=pltpu.CompilerParams(
            collective_id=0, has_side_effects=True, vmem_limit_bytes=56 * 2**20
        ),
        cost_estimate=pl.CostEstimate(
            flops=16 * 2**30, bytes_accessed=10 * 2**20, transcendentals=4 * 2**20
        ),
    )(key_rows, value_rows, queries, rates, fast_one, fast_three, fast_two, head_gain)


def solution(mesh):
    ctx, head = mesh.shape["ctx"], mesh.shape["head"]
    def run(*args):
        members = args[4].shape[0] // head
        split = Mesh(mesh.devices.reshape(ctx // members, members, head), ("grp", "mem", "head"))
        rows = P(("grp", "mem"), "head")
        weights = P("head", None, None)
        groups, width, rows_here = ctx // members, args[4].shape[1], args[0].shape[0] // ctx
        whole_blocks = rows_here % 64 == 0 and width % 128 == 0 and members * rows_here > WINDOW
        fits = whole_blocks and members > 1 and groups % 2 == 0 and 3 * width // 128 >= members
        return jax.shard_map(
            local_kernel if fits and head == 1 else local,
            mesh=split,
            in_specs=(rows, rows, rows, rows, weights, weights, weights, P("head")),
            out_specs=(rows, rows),
            check_vma=False,
        )(*args)

    return run
```

```python
import functools

import jax
import jax.numpy as jnp
from jax import lax
from jax.experimental import pallas as pl
from jax.experimental.pallas import tpu as pltpu
from jax.sharding import Mesh
from jax.sharding import PartitionSpec as P

WINDOW = 1024
NS_STEPS = 2

COEF_A = 3.4445
COEF_B = -4.775
COEF_C = 2.0315
EPSILON = 1e-06


def rms_heads(block):
    return block / jnp.sqrt(jnp.mean(block * block, axis=-1, keepdims=True) + EPSILON)


def to_heads(rows):
    return lax.all_to_all(rows, "mem", split_axis=1, concat_axis=0, tiled=True)


def to_tokens(rows):
    return lax.all_to_all(rows, "mem", split_axis=0, concat_axis=1, tiled=True)


def with_earlier(rows):
    tokens, groups = rows.shape[0], lax.axis_size("grp")
    parts, missing, distance = [rows], WINDOW, 1
    while missing > 0:
        take = min(missing, tokens)
        pairs = [(i, i + distance) for i in range(groups - distance)]
        parts.insert(0, lax.ppermute(rows[tokens - take :], "grp", pairs))
        missing -= take
        distance += 1
    return jnp.concatenate(parts, axis=0)


def window_attention(q, k, v):
    tokens, width = q.shape
    block = 512 if tokens % 512 == 0 else tokens
    count = tokens // block
    keys, values = with_earlier(k), with_earlier(v)
    reach = WINDOW + block
    keys = jnp.stack([keys[i * block : i * block + reach] for i in range(count)])
    values = jnp.stack([values[i * block : i * block + reach] for i in range(count)])
    scores = jnp.einsum(
        "bqd,bkd->bqk", q.reshape(count, block, width), keys, preferred_element_type=jnp.float32
    ) * width ** (-0.5)
    query_pos = lax.broadcasted_iota(jnp.int32, (count, block, reach), 1) + WINDOW
    key_pos = lax.broadcasted_iota(jnp.int32, (count, block, reach), 2)
    base = lax.broadcasted_iota(jnp.int32, (count, block, reach), 0) * block
    first_key = lax.axis_index("grp") * tokens - WINDOW
    offset = query_pos - key_pos
    allowed = (offset >= 0) & (offset < WINDOW) & (key_pos + base + first_key >= 0)
    scores = jnp.where(allowed, scores, -1e30)
    row_top = jnp.max(scores, axis=-1, keepdims=True)
    exponent = jnp.exp(scores - row_top)
    weights = (exponent / jnp.sum(exponent, axis=-1, keepdims=True)).astype(jnp.bfloat16)
    out = jnp.einsum("bqk,bkd->bqd", weights, values, preferred_element_type=jnp.float32)
    return out.reshape(tokens, width)


def orthogonal(gradient):
    squares = jnp.sum(gradient * gradient)
    current = (gradient / (jnp.sqrt(squares) + 1e-07)).astype(jnp.bfloat16)
    for sweep_index in range(NS_STEPS):
        gram = jnp.einsum(
            "rc,sc->rs", current, current, preferred_element_type=jnp.float32
        ).astype(jnp.bfloat16)
        mixer = (
            COEF_B * gram.astype(jnp.float32)
            + COEF_C * jnp.dot(gram, gram, preferred_element_type=jnp.float32)
        ).astype(jnp.bfloat16)
        current = (
            COEF_A * current.astype(jnp.float32)
            + jnp.dot(mixer, current, preferred_element_type=jnp.float32)
        ).astype(jnp.bfloat16)
    return current


def fast_weights(q, k, v, rates, one, three, two):
    f32 = jnp.float32
    key_normed = rms_heads(k.astype(f32)).astype(jnp.bfloat16)
    query_normed = rms_heads(q.astype(f32)).astype(jnp.bfloat16)
    hidden_one = jnp.dot(key_normed, one, preferred_element_type=f32)
    hidden_three = jnp.dot(key_normed, three, preferred_element_type=f32)
    sigmoid_one = jax.nn.sigmoid(hidden_one)
    active = hidden_one * sigmoid_one
    hidden = (active * hidden_three).astype(jnp.bfloat16)
    delta_out = (-rates * v.astype(f32)).astype(jnp.bfloat16)
    delta_hidden = jnp.einsum("td,fd->tf", delta_out, two, preferred_element_type=f32)
    delta_three = (delta_hidden * active).astype(jnp.bfloat16)
    delta_one = (
        delta_hidden * hidden_three * sigmoid_one * (1.0 + hidden_one * (1.0 - sigmoid_one))
    ).astype(jnp.bfloat16)
    gradient_one = jnp.einsum("td,tf->df", key_normed, delta_one, preferred_element_type=f32)
    gradient_three = jnp.einsum("td,tf->df", key_normed, delta_three, preferred_element_type=f32)
    gradient_two = jnp.einsum("tf,td->fd", hidden, delta_out, preferred_element_type=f32)
    grads = lax.psum(jnp.stack([gradient_one, gradient_three, gradient_two]), "grp")
    new = [
        (old.astype(f32) - orthogonal(grads[i]).astype(f32)).astype(jnp.bfloat16)
        for i, old in enumerate((one, three, two))
    ]
    query_one = jnp.dot(query_normed, new[0], preferred_element_type=f32)
    query_three = jnp.dot(query_normed, new[1], preferred_element_type=f32)
    query_hidden = (jax.nn.silu(query_one) * query_three).astype(jnp.bfloat16)
    return jnp.dot(query_hidden, new[2], preferred_element_type=f32)


def normed(rows):
    rows = rows.astype(jnp.float32)
    heads = lax.axis_size("head")
    total = lax.psum(jnp.sum(rows * rows, axis=1, keepdims=True), "head")
    return (rows / jnp.sqrt(total / (rows.shape[1] * heads) + EPSILON)).astype(jnp.bfloat16)


def local(queries, key_rows, value_rows, token_rates, fast_one, fast_three, fast_two, head_gain):
    me = lax.axis_index("mem")
    k, v, q = to_heads(key_rows), to_heads(value_rows), to_heads(queries)
    first = lax.axis_index("head") * head_gain.shape[0] if token_rates.shape[1] != head_gain.shape[0] else 0
    rates = lax.all_gather(token_rates, "mem", axis=0, tiled=True)
    rates = lax.dynamic_slice_in_dim(rates, me + first, 1, axis=1)
    one, three, two = (
        lax.dynamic_index_in_dim(w, me, 0, keepdims=False) for w in (fast_one, fast_three, fast_two)
    )
    gain = lax.dynamic_index_in_dim(head_gain, me, 0, keepdims=False)
    attended = window_attention(q, k, v)
    fast = fast_weights(q, k, v, rates, one, three, two) * gain
    window_rows = to_tokens(attended.astype(jnp.bfloat16))
    fast_rows = to_tokens(fast.astype(jnp.bfloat16))
    return normed(window_rows), normed(fast_rows)


def dot_nn(a, b):
    return jnp.dot(a, b, preferred_element_type=jnp.float32)


def dot_nt(a, b):
    return lax.dot_general(a, b, (((1,), (1,)), ((), ())), preferred_element_type=jnp.float32)


def dot_tn(a, b):
    return lax.dot_general(a, b, (((0,), (0,)), ((), ())), preferred_element_type=jnp.float32)


def other_member(a, b, count):
    out, bit = 0, 1
    while bit < count:
        out = out + bit * lax.rem(a // bit + b // bit, 2)
        bit *= 2
    return out


def layer_kernel(
    dims, k_hbm, v_hbm, q_hbm, rates_hbm, one_hbm, three_hbm, two_hbm, gain_ref,
    window_recv, fast_recv,
    kbuf, vbuf, qbuf, rbuf, weights, updated, grads, from_outer, from_inner, to_inner, to_outer,
    window_send, fast_send,
    k_s, k_r, v_s, v_r, q_s, q_r, r_s, r_r, halo_s, halo_r, outer_r, inner_r, inner_s, outer_s,
    win_s, win_r, fast_s, fast_r, load_sem,
):
    groups, members, rows, width, pad, chunk = dims
    f32, bf16 = jnp.float32, jnp.bfloat16
    me, grp = lax.axis_index("mem"), lax.axis_index("grp")
    base = pad + WINDOW
    reach = base + rows
    stretch = members * rows
    chunks = 3 * width // chunk
    halo_first = (stretch - WINDOW) // rows
    halo_part = (halo_first + 1) * rows - (stretch - WINDOW)
    has_lower, has_upper = grp > 0, grp < groups - 1
    has_outer = jnp.logical_and(has_lower, has_upper)
    in_lower = grp < groups // 2
    inner = jnp.where(in_lower, grp + 1, grp - 1)
    outer = jnp.where(in_lower, grp - 1, grp + 1)
    is_mid = jnp.logical_or(grp == groups // 2 - 1, grp == groups // 2)

    barrier = pltpu.get_barrier_semaphore()
    for d in range(1, members):
        pl.semaphore_signal(barrier, inc=1, device_id={"mem": lax.rem(me + d, members)})

    @pl.when(has_lower)
    def _():
        pl.semaphore_signal(barrier, inc=1, device_id={"grp": grp - 1})

    @pl.when(has_upper)
    def _():
        pl.semaphore_signal(barrier, inc=1, device_id={"grp": grp + 1})

    pl.semaphore_wait(
        barrier, members - 1 + jnp.minimum(grp, 1) + jnp.minimum(groups - 1 - grp, 1)
    )

    def cols(p):
        return pl.ds(pl.multiple_of(p * width, width), width)

    def own_rows(s, first=base):
        return pl.ds(pl.multiple_of(first + s * rows, 16), rows)

    def exchange(hbm, buf, first, send, recv, d):
        peer = other_member(me, d, members)
        return pltpu.make_async_remote_copy(
            src_ref=hbm.at[:, cols(peer)], dst_ref=buf.at[own_rows(me, first)],
            send_sem=send.at[d], recv_sem=recv.at[d], device_id={"mem": peer},
        )

    def kept(hbm, buf, first, recv):
        return pltpu.make_async_copy(
            hbm.at[:, cols(me)], buf.at[own_rows(me, first)], recv.at[0]
        )

    def rates_to(d):
        peer = other_member(me, d, members)
        return pltpu.make_async_remote_copy(
            src_ref=rates_hbm, dst_ref=rbuf.at[me],
            send_sem=r_s.at[d], recv_sem=r_r.at[d], device_id={"mem": peer},
        )

    def block_to(send_buf, recv_buf, send, recv, s):
        d = other_member(me, s, members)
        return pltpu.make_async_remote_copy(
            src_ref=send_buf.at[s], dst_ref=recv_buf.at[me],
            send_sem=send.at[d], recv_sem=recv.at[d], device_id={"mem": s},
        )

    def block_kept(send_buf, recv_buf, recv):
        return pltpu.make_async_copy(send_buf.at[me], recv_buf.at[me], recv.at[0])

    own_rates = pltpu.make_async_copy(rates_hbm, rbuf.at[me], r_r.at[0])
    own_rates.start()
    kept(k_hbm, kbuf, base, k_r).start()
    kept(v_hbm, vbuf, base, v_r).start()
    kept(q_hbm, qbuf, 0, q_r).start()

    @pl.loop(1, members)
    def _(d):
        exchange(k_hbm, kbuf, base, k_s, k_r, d).start()

        @pl.when(d == 1)
        def _():
            exchange(v_hbm, vbuf, base, v_s, v_r, d).start()

    @pl.loop(1, members)
    def _(d):
        rates_to(d).start()

    loads = [
        pltpu.make_async_copy(hbm.at[me], weights.at[i], load_sem.at[i])
        for i, hbm in enumerate((one_hbm, three_hbm, two_hbm))
    ]
    for load in loads:
        load.start()
    kbuf[0:pad] = jnp.zeros((pad, width), bf16)
    vbuf[0:pad] = jnp.zeros((pad, width), bf16)

    @pl.when(grp == 0)
    def _():
        kbuf[pad:base] = jnp.zeros((WINDOW, width), bf16)
        vbuf[pad:base] = jnp.zeros((WINDOW, width), bf16)

    grads[...] = jnp.zeros_like(grads)
    for load in loads:
        load.wait()

    def halo_copy(which, s, size):
        buf = (kbuf, vbuf)[which]
        start = base + s * rows + rows - size
        return pltpu.make_async_remote_copy(
            src_ref=buf.at[pl.ds(pl.multiple_of(start, 16), size)],
            dst_ref=buf.at[pl.ds(pl.multiple_of(start - stretch, 16), size)],
            send_sem=halo_s.at[which, s], recv_sem=halo_r.at[which, s],
            device_id={"grp": grp + 1},
        )

    def for_halo(which, s, present, act):
        @pl.when(jnp.logical_and(present, s == halo_first))
        def _():
            act(halo_copy(which, s, halo_part))

        @pl.when(jnp.logical_and(present, s > halo_first))
        def _():
            act(halo_copy(which, s, rows))

    def rms_unit(x):
        x = x.astype(f32)
        return (x * lax.rsqrt(jnp.mean(x * x, axis=1, keepdims=True) + EPSILON)).astype(bf16)

    @pl.loop(0, members)
    def _(d):
        s = other_member(me, d, members)

        @pl.when(d == 0)
        def _():
            kept(k_hbm, kbuf, base, k_r).wait()

        @pl.when(d > 0)
        def _():
            exchange(k_hbm, kbuf, base, k_s, k_r, d).wait_recv()

        for_halo(0, s, has_upper, lambda copy: copy.start())

        @pl.when(d > 1)
        def _():
            exchange(v_hbm, vbuf, base, v_s, v_r, d).start()

        @pl.when(d == 0)
        def _():
            kept(v_hbm, vbuf, base, v_r).wait()

        @pl.when(d == 1)
        def _():
            exchange(v_hbm, vbuf, base, v_s, v_r, d).wait_recv()

        for_halo(1, s, jnp.logical_and(has_upper, d < 2), lambda copy: copy.start())

    @pl.loop(0, members)
    def _(d):
        s = other_member(me, d, members)

        @pl.when(d == 0)
        def _():
            own_rates.wait()

        @pl.when(d > 0)
        def _():
            rates_to(d).wait_recv()

        @pl.when(d > 1)
        def _():
            exchange(v_hbm, vbuf, base, v_s, v_r, d).wait_recv()

        for_halo(1, s, jnp.logical_and(has_upper, d > 1), lambda copy: copy.start())

        @pl.when(d > 0)
        def _():
            exchange(q_hbm, qbuf, 0, q_s, q_r, d).start()

        key_unit = rms_unit(kbuf[own_rows(s)])
        heads_rates = rbuf[s]
        is_mine = lax.broadcasted_iota(jnp.int32, heads_rates.shape, 0) == me
        rate_row = jnp.sum(jnp.where(is_mine, heads_rates, 0.0), axis=0, keepdims=True)
        diagonal = lax.broadcasted_iota(jnp.int32, (rows, rows), 0) == lax.broadcasted_iota(
            jnp.int32, (rows, rows), 1
        )
        rate = jnp.sum(jnp.where(diagonal, rate_row, 0.0), axis=1, keepdims=True)
        delta_out = (-rate * vbuf[own_rows(s)].astype(f32)).astype(bf16)
        a = dot_nn(key_unit, weights[0])
        b = dot_nn(key_unit, weights[1])
        dh = dot_nt(delta_out, weights[2])
        sig = 1.0 / (1.0 + jnp.exp(-a))
        active = a * sig
        hidden = (active * b).astype(bf16)
        delta_three = (dh * active).astype(bf16)
        delta_one = (dh * b * sig * (1.0 + a * (1.0 - sig))).astype(bf16)
        grads[0:width] += dot_tn(key_unit, delta_one)
        grads[width : 2 * width] += dot_tn(key_unit, delta_three)
        grads[2 * width : 3 * width] += dot_tn(hidden, delta_out)

    def rows_of(i):
        return pl.ds(pl.multiple_of(i * chunk, chunk), chunk)

    def inward(i, target, recv):
        return pltpu.make_async_remote_copy(
            src_ref=to_inner.at[i], dst_ref=target.at[i],
            send_sem=inner_s.at[i], recv_sem=recv.at[i], device_id={"grp": inner},
        )

    def outward(i):
        return pltpu.make_async_remote_copy(
            src_ref=to_outer.at[i], dst_ref=from_inner.at[i],
            send_sem=outer_s.at[i], recv_sem=inner_r.at[i], device_id={"grp": outer},
        )

    def send_inward(i):
        @pl.when(is_mid)
        def _():
            inward(i, from_inner, inner_r).start()

        @pl.when(jnp.logical_not(is_mid))
        def _():
            inward(i, from_outer, outer_r).start()

    @pl.when(jnp.logical_not(has_outer))
    def _():
        @pl.loop(0, chunks)
        def _(i):
            to_inner[i] = grads[rows_of(i)].astype(bf16)
            send_inward(i)

    def attend(s):
        scores = dot_nt(qbuf[own_rows(s, 0)], kbuf[pl.ds(pl.multiple_of(s * rows, 16), reach)])
        scores = scores * width ** (-0.5)
        query = lax.broadcasted_iota(jnp.int32, (rows, reach), 0)
        key = lax.broadcasted_iota(jnp.int32, (rows, reach), 1)
        offset = query - key + base
        first = grp * stretch + s * rows - base
        allowed = (offset >= 0) & (offset < WINDOW) & (key + first >= 0)
        scores = jnp.where(allowed, scores, -1e30)
        top = jnp.max(scores, axis=1, keepdims=True)
        exponent = jnp.exp(scores - top)
        total = jnp.sum(exponent, axis=1, keepdims=True)
        out = dot_nn(
            exponent.astype(bf16), vbuf[pl.ds(pl.multiple_of(s * rows, 16), reach)]
        )
        return (out / total).astype(bf16)

    def orthogonal_update(m):
        gradient = grads[pl.ds(pl.multiple_of(m * width, width), width)]
        squares = jnp.sum(jnp.sum(gradient * gradient, axis=1, keepdims=True), axis=0, keepdims=True)
        current = (gradient / (jnp.sqrt(squares) + 1e-07)).astype(bf16)
        for sweep_index in range(NS_STEPS):
            gram = dot_nt(current, current).astype(bf16)
            mixer = (COEF_B * gram.astype(f32) + COEF_C * dot_nn(gram, gram)).astype(bf16)
            current = (COEF_A * current.astype(f32) + dot_nn(mixer, current)).astype(bf16)
        updated[m] = (weights[m].astype(f32) - current.astype(f32)).astype(bf16)

    per_matrix = width // chunk
    lag = 2

    @pl.loop(0, chunks + lag)
    def _(i):
        @pl.when(jnp.logical_and(has_outer, i < chunks))
        def _():
            inward(i, from_outer, outer_r).wait_recv()
            partial = grads[rows_of(i)] + from_outer[i].astype(f32)
            to_inner[i] = partial.astype(bf16)
            send_inward(i)

        @pl.when(i >= lag)
        def _():
            j = i - lag
            outward(j).wait_recv()

            @pl.when(is_mid)
            def _():
                grads[rows_of(j)] = to_inner[j].astype(f32) + from_inner[j].astype(f32)

            @pl.when(jnp.logical_not(is_mid))
            def _():
                grads[rows_of(j)] = from_inner[j].astype(f32)

            @pl.when(has_outer)
            def _():
                to_outer[j] = grads[rows_of(j)].astype(bf16)
                outward(j).start()

            @pl.when(lax.rem(j, per_matrix) == per_matrix - 1)
            def _():
                orthogonal_update(j // per_matrix)

        @pl.when(jnp.logical_and(i >= chunks - members, i < chunks))
        def _():
            s = chunks - 1 - i
            d = other_member(me, s, members)

            @pl.when(d == 0)
            def _():
                kept(q_hbm, qbuf, 0, q_r).wait()

            @pl.when(d > 0)
            def _():
                exchange(q_hbm, qbuf, 0, q_s, q_r, d).wait_recv()

            piece = s + halo_first
            for which in range(2):
                for_halo(
                    which, piece, jnp.logical_and(has_lower, piece < members),
                    lambda copy: copy.wait_recv(),
                )
            window_send[s] = attend(s)

            @pl.when(s == me)
            def _():
                block_kept(window_send, window_recv, win_r).start()

            @pl.when(s != me)
            def _():
                block_to(window_send, window_recv, win_s, win_r, s).start()

    gain = gain_ref[me]

    @pl.loop(0, members)
    def _(d):
        s = other_member(me, members - 1 - d, members)
        unit = rms_unit(qbuf[own_rows(s, 0)])
        a = dot_nn(unit, updated[0])
        b = dot_nn(unit, updated[1])
        hidden = (a / (1.0 + jnp.exp(-a)) * b).astype(bf16)
        fast_send[s] = (dot_nn(hidden, updated[2]) * gain).astype(bf16)

        @pl.when(s == me)
        def _():
            block_kept(fast_send, fast_recv, fast_r).start()

        @pl.when(s != me)
        def _():
            block_to(fast_send, fast_recv, fast_s, fast_r, s).start()

    block_kept(window_send, window_recv, win_r).wait()
    block_kept(fast_send, fast_recv, fast_r).wait()

    @pl.loop(1, members)
    def _(d):
        s = other_member(me, d, members)
        block_to(window_send, window_recv, win_s, win_r, s).wait_recv()
        block_to(fast_send, fast_recv, fast_s, fast_r, s).wait_recv()

    @pl.loop(1, members)
    def _(d):
        s = other_member(me, d, members)
        rates_to(d).wait_send()
        exchange(k_hbm, kbuf, base, k_s, k_r, d).wait_send()
        exchange(v_hbm, vbuf, base, v_s, v_r, d).wait_send()
        exchange(q_hbm, qbuf, 0, q_s, q_r, d).wait_send()
        block_to(window_send, window_recv, win_s, win_r, s).wait_send()
        block_to(fast_send, fast_recv, fast_s, fast_r, s).wait_send()

    @pl.loop(0, members)
    def _(s):
        for which in range(2):
            for_halo(which, s, has_upper, lambda copy: copy.wait_send())

    @pl.loop(0, chunks)
    def _(i):
        inward(i, from_inner, inner_r).wait_send()

        @pl.when(has_outer)
        def _():
            outward(i).wait_send()


def norm_kernel(window_raw, fast_raw, window_ref, fast_ref):
    heads, _, width = window_raw.shape
    for raw, out in ((window_raw, window_ref), (fast_raw, fast_ref)):
        total = 0.0
        for h in range(heads):
            x = raw[h].astype(jnp.float32)
            total = total + jnp.sum(x * x, axis=1, keepdims=True)
        scale = lax.rsqrt(total / (heads * width) + EPSILON)
        for h in range(heads):
            out[:, h * width : (h + 1) * width] = (raw[h].astype(jnp.float32) * scale).astype(
                jnp.bfloat16
            )


def normed_rows(window_raw, fast_raw):
    heads, rows, width = window_raw.shape
    block = 64
    raw = pl.BlockSpec((heads, block, width), lambda i: (0, i, 0))
    done = pl.BlockSpec((block, heads * width), lambda i: (i, 0))
    out = jax.ShapeDtypeStruct((rows, heads * width), jnp.bfloat16)
    return pl.pallas_call(
        norm_kernel,
        grid=(rows // block,),
        out_shape=(out, out),
        in_specs=[raw, raw],
        out_specs=(done, done),
        compiler_params=pltpu.CompilerParams(vmem_limit_bytes=60 * 2**20),
        cost_estimate=pl.CostEstimate(
            flops=8 * rows * heads * width, bytes_accessed=8 * rows * heads * width, transcendentals=0
        ),
    )(window_raw, fast_raw)


def local_kernel(queries, key_rows, value_rows, token_rates, fast_one, fast_three, fast_two, head_gain):
    groups, members = lax.axis_size("grp"), lax.axis_size("mem")
    rows, width = queries.shape[0], fast_one.shape[1]
    pad = -(WINDOW + rows) % 128
    chunk = 128
    chunks = 3 * width // chunk
    bf16, dma = jnp.bfloat16, pltpu.SemaphoreType.DMA
    keys = pltpu.VMEM((pad + WINDOW + members * rows, width), bf16)
    parts = pltpu.VMEM((chunks, chunk, width), bf16)
    blocks = pltpu.VMEM((members, rows, width), bf16)
    matrices = pltpu.VMEM((3, width, width), bf16)
    anywhere = pl.BlockSpec(memory_space=pl.ANY)
    out = jax.ShapeDtypeStruct((members, rows, width), bf16)
    window_raw, fast_raw = pl.pallas_call(
        functools.partial(layer_kernel, (groups, members, rows, width, pad, chunk)),
        out_shape=(out, out),
        in_specs=[anywhere] * 7 + [pl.BlockSpec(memory_space=pltpu.SMEM)],
        out_specs=(anywhere, anywhere),
        scratch_shapes=[
            keys, keys, pltpu.VMEM((members * rows, width), bf16),
            pltpu.VMEM((members, members, rows), jnp.float32),
            matrices, matrices, pltpu.VMEM((3 * width, width), jnp.float32),
            parts, parts, parts, parts, blocks, blocks,
        ]
        + [dma((members,))] * 8
        + [dma((2, members))] * 2
        + [dma((chunks,))] * 4
        + [dma((members,))] * 4
        + [dma((3,))],
        compiler_params=pltpu.CompilerParams(
            collective_id=0, has_side_effects=True, vmem_limit_bytes=56 * 2**20
        ),
        cost_estimate=pl.CostEstimate(
            flops=16 * 2**30, bytes_accessed=10 * 2**20, transcendentals=4 * 2**20
        ),
    )(key_rows, value_rows, queries, token_rates.T, fast_one, fast_three, fast_two, head_gain)
    return normed_rows(window_raw, fast_raw)


def solution(mesh):
    ctx, head = mesh.shape["ctx"], mesh.shape["head"]
    def run(*args):
        members = args[4].shape[0] // head
        split = Mesh(mesh.devices.reshape(ctx // members, members, head), ("grp", "mem", "head"))
        rows = P(("grp", "mem"), "head")
        weights = P("head", None, None)
        groups, width, rows_here = ctx // members, args[4].shape[1], args[0].shape[0] // ctx
        whole_blocks = rows_here % 64 == 0 and width % 128 == 0 and members * rows_here > WINDOW
        pairs = groups % 2 == 0 and members > 1 and members & (members - 1) == 0
        fits = whole_blocks and pairs and members % 8 == 0 and 3 * width // 128 >= members
        return jax.shard_map(
            local_kernel if fits and head == 1 else local,
            mesh=split,
            in_specs=(rows, rows, rows, rows, weights, weights, weights, P("head")),
            out_specs=(rows, rows),
            check_vma=False,
        )(*args)

    return run
```

```python
import functools

import jax
import jax.numpy as jnp
from jax import lax
from jax.experimental import pallas as pl
from jax.experimental.pallas import tpu as pltpu
from jax.sharding import Mesh
from jax.sharding import PartitionSpec as P

WINDOW = 1024
NS_STEPS = 2

COEF_A = 3.4445
COEF_B = -4.775
COEF_C = 2.0315
EPSILON = 1e-06


def rms_heads(block):
    return block / jnp.sqrt(jnp.mean(block * block, axis=-1, keepdims=True) + EPSILON)


def to_heads(rows):
    return lax.all_to_all(rows, "mem", split_axis=1, concat_axis=0, tiled=True)


def to_tokens(rows):
    return lax.all_to_all(rows, "mem", split_axis=0, concat_axis=1, tiled=True)


def with_earlier(rows):
    tokens, groups = rows.shape[0], lax.axis_size("grp")
    parts, missing, distance = [rows], WINDOW, 1
    while missing > 0:
        take = min(missing, tokens)
        pairs = [(i, i + distance) for i in range(groups - distance)]
        parts.insert(0, lax.ppermute(rows[tokens - take :], "grp", pairs))
        missing -= take
        distance += 1
    return jnp.concatenate(parts, axis=0)


def window_attention(q, k, v):
    tokens, width = q.shape
    block = 512 if tokens % 512 == 0 else tokens
    count = tokens // block
    keys, values = with_earlier(k), with_earlier(v)
    reach = WINDOW + block
    keys = jnp.stack([keys[i * block : i * block + reach] for i in range(count)])
    values = jnp.stack([values[i * block : i * block + reach] for i in range(count)])
    scores = jnp.einsum(
        "bqd,bkd->bqk", q.reshape(count, block, width), keys, preferred_element_type=jnp.float32
    ) * width ** (-0.5)
    query_pos = lax.broadcasted_iota(jnp.int32, (count, block, reach), 1) + WINDOW
    key_pos = lax.broadcasted_iota(jnp.int32, (count, block, reach), 2)
    base = lax.broadcasted_iota(jnp.int32, (count, block, reach), 0) * block
    first_key = lax.axis_index("grp") * tokens - WINDOW
    offset = query_pos - key_pos
    allowed = (offset >= 0) & (offset < WINDOW) & (key_pos + base + first_key >= 0)
    scores = jnp.where(allowed, scores, -1e30)
    row_top = jnp.max(scores, axis=-1, keepdims=True)
    exponent = jnp.exp(scores - row_top)
    weights = (exponent / jnp.sum(exponent, axis=-1, keepdims=True)).astype(jnp.bfloat16)
    out = jnp.einsum("bqk,bkd->bqd", weights, values, preferred_element_type=jnp.float32)
    return out.reshape(tokens, width)


def orthogonal(gradient):
    squares = jnp.sum(gradient * gradient)
    current = (gradient / (jnp.sqrt(squares) + 1e-07)).astype(jnp.bfloat16)
    for sweep_index in range(NS_STEPS):
        gram = jnp.einsum(
            "rc,sc->rs", current, current, preferred_element_type=jnp.float32
        ).astype(jnp.bfloat16)
        mixer = (
            COEF_B * gram.astype(jnp.float32)
            + COEF_C * jnp.dot(gram, gram, preferred_element_type=jnp.float32)
        ).astype(jnp.bfloat16)
        current = (
            COEF_A * current.astype(jnp.float32)
            + jnp.dot(mixer, current, preferred_element_type=jnp.float32)
        ).astype(jnp.bfloat16)
    return current


def fast_weights(q, k, v, rates, one, three, two):
    f32 = jnp.float32
    key_normed = rms_heads(k.astype(f32)).astype(jnp.bfloat16)
    query_normed = rms_heads(q.astype(f32)).astype(jnp.bfloat16)
    hidden_one = jnp.dot(key_normed, one, preferred_element_type=f32)
    hidden_three = jnp.dot(key_normed, three, preferred_element_type=f32)
    sigmoid_one = jax.nn.sigmoid(hidden_one)
    active = hidden_one * sigmoid_one
    hidden = (active * hidden_three).astype(jnp.bfloat16)
    delta_out = (-rates * v.astype(f32)).astype(jnp.bfloat16)
    delta_hidden = jnp.einsum("td,fd->tf", delta_out, two, preferred_element_type=f32)
    delta_three = (delta_hidden * active).astype(jnp.bfloat16)
    delta_one = (
        delta_hidden * hidden_three * sigmoid_one * (1.0 + hidden_one * (1.0 - sigmoid_one))
    ).astype(jnp.bfloat16)
    gradient_one = jnp.einsum("td,tf->df", key_normed, delta_one, preferred_element_type=f32)
    gradient_three = jnp.einsum("td,tf->df", key_normed, delta_three, preferred_element_type=f32)
    gradient_two = jnp.einsum("tf,td->fd", hidden, delta_out, preferred_element_type=f32)
    grads = lax.psum(jnp.stack([gradient_one, gradient_three, gradient_two]), "grp")
    new = [
        (old.astype(f32) - orthogonal(grads[i]).astype(f32)).astype(jnp.bfloat16)
        for i, old in enumerate((one, three, two))
    ]
    query_one = jnp.dot(query_normed, new[0], preferred_element_type=f32)
    query_three = jnp.dot(query_normed, new[1], preferred_element_type=f32)
    query_hidden = (jax.nn.silu(query_one) * query_three).astype(jnp.bfloat16)
    return jnp.dot(query_hidden, new[2], preferred_element_type=f32)


def normed(rows):
    rows = rows.astype(jnp.float32)
    heads = lax.axis_size("head")
    total = lax.psum(jnp.sum(rows * rows, axis=1, keepdims=True), "head")
    return (rows / jnp.sqrt(total / (rows.shape[1] * heads) + EPSILON)).astype(jnp.bfloat16)


def local(queries, key_rows, value_rows, token_rates, fast_one, fast_three, fast_two, head_gain):
    me = lax.axis_index("mem")
    k, v, q = to_heads(key_rows), to_heads(value_rows), to_heads(queries)
    first = lax.axis_index("head") * head_gain.shape[0] if token_rates.shape[1] != head_gain.shape[0] else 0
    rates = lax.all_gather(token_rates, "mem", axis=0, tiled=True)
    rates = lax.dynamic_slice_in_dim(rates, me + first, 1, axis=1)
    one, three, two = (
        lax.dynamic_index_in_dim(w, me, 0, keepdims=False) for w in (fast_one, fast_three, fast_two)
    )
    gain = lax.dynamic_index_in_dim(head_gain, me, 0, keepdims=False)
    attended = window_attention(q, k, v)
    fast = fast_weights(q, k, v, rates, one, three, two) * gain
    window_rows = to_tokens(attended.astype(jnp.bfloat16))
    fast_rows = to_tokens(fast.astype(jnp.bfloat16))
    return normed(window_rows), normed(fast_rows)


def dot_nn(a, b):
    return jnp.dot(a, b, preferred_element_type=jnp.float32)


def dot_nt(a, b):
    return lax.dot_general(a, b, (((1,), (1,)), ((), ())), preferred_element_type=jnp.float32)


def dot_tn(a, b):
    return lax.dot_general(a, b, (((0,), (0,)), ((), ())), preferred_element_type=jnp.float32)


def other_member(a, b, count):
    out, bit = 0, 1
    while bit < count:
        out = out + bit * lax.rem(a // bit + b // bit, 2)
        bit *= 2
    return out


def layer_kernel(
    dims, k_hbm, v_hbm, q_hbm, rates_hbm, one_hbm, three_hbm, two_hbm, gain_ref,
    window_recv, fast_recv,
    kbuf, vbuf, qbuf, rbuf, weights, updated, grads, from_outer, from_inner, to_inner, to_outer,
    window_send, fast_send, units, hiddens, gates, slopes,
    k_s, k_r, v_s, v_r, q_s, q_r, r_s, r_r, halo_s, halo_r, outer_r, inner_r, inner_s, outer_s,
    win_s, win_r, fast_s, fast_r, load_sem,
):
    groups, members, rows, width, pad, chunk = dims
    f32, bf16 = jnp.float32, jnp.bfloat16
    me, grp = lax.axis_index("mem"), lax.axis_index("grp")
    base = pad + WINDOW
    reach = base + rows
    stretch = members * rows
    chunks = 3 * width // chunk
    halo_first = (stretch - WINDOW) // rows
    halo_part = (halo_first + 1) * rows - (stretch - WINDOW)
    has_lower, has_upper = grp > 0, grp < groups - 1
    has_outer = jnp.logical_and(has_lower, has_upper)
    in_lower = grp < groups // 2
    inner = jnp.where(in_lower, grp + 1, grp - 1)
    outer = jnp.where(in_lower, grp - 1, grp + 1)
    is_mid = jnp.logical_or(grp == groups // 2 - 1, grp == groups // 2)

    barrier = pltpu.get_barrier_semaphore()
    for d in range(1, members):
        pl.semaphore_signal(barrier, inc=1, device_id={"mem": lax.rem(me + d, members)})

    @pl.when(has_lower)
    def _():
        pl.semaphore_signal(barrier, inc=1, device_id={"grp": grp - 1})

    @pl.when(has_upper)
    def _():
        pl.semaphore_signal(barrier, inc=1, device_id={"grp": grp + 1})

    pl.semaphore_wait(
        barrier, members - 1 + jnp.minimum(grp, 1) + jnp.minimum(groups - 1 - grp, 1)
    )

    def cols(p):
        return pl.ds(pl.multiple_of(p * width, width), width)

    def own_rows(s, first=base):
        return pl.ds(pl.multiple_of(first + s * rows, 16), rows)

    def exchange(hbm, buf, first, send, recv, d):
        peer = other_member(me, d, members)
        return pltpu.make_async_remote_copy(
            src_ref=hbm.at[:, cols(peer)], dst_ref=buf.at[own_rows(me, first)],
            send_sem=send.at[d], recv_sem=recv.at[d], device_id={"mem": peer},
        )

    def kept(hbm, buf, first, recv):
        return pltpu.make_async_copy(
            hbm.at[:, cols(me)], buf.at[own_rows(me, first)], recv.at[0]
        )

    def rates_to(d):
        peer = other_member(me, d, members)
        return pltpu.make_async_remote_copy(
            src_ref=rates_hbm, dst_ref=rbuf.at[me],
            send_sem=r_s.at[d], recv_sem=r_r.at[d], device_id={"mem": peer},
        )

    def block_to(send_buf, recv_buf, send, recv, s):
        d = other_member(me, s, members)
        return pltpu.make_async_remote_copy(
            src_ref=send_buf.at[s], dst_ref=recv_buf.at[me],
            send_sem=send.at[d], recv_sem=recv.at[d], device_id={"mem": s},
        )

    def block_kept(send_buf, recv_buf, recv):
        return pltpu.make_async_copy(send_buf.at[me], recv_buf.at[me], recv.at[0])

    own_rates = pltpu.make_async_copy(rates_hbm, rbuf.at[me], r_r.at[0])
    own_rates.start()
    kept(k_hbm, kbuf, base, k_r).start()
    kept(v_hbm, vbuf, base, v_r).start()
    kept(q_hbm, qbuf, 0, q_r).start()

    @pl.loop(1, members)
    def _(d):
        exchange(k_hbm, kbuf, base, k_s, k_r, d).start()

        @pl.when(d == 1)
        def _():
            exchange(v_hbm, vbuf, base, v_s, v_r, d).start()

    @pl.loop(1, members)
    def _(d):
        rates_to(d).start()

    loads = [
        pltpu.make_async_copy(hbm.at[me], weights.at[i], load_sem.at[i])
        for i, hbm in enumerate((one_hbm, three_hbm, two_hbm))
    ]
    for load in loads:
        load.start()
    kbuf[0:pad] = jnp.zeros((pad, width), bf16)
    vbuf[0:pad] = jnp.zeros((pad, width), bf16)

    @pl.when(grp == 0)
    def _():
        kbuf[pad:base] = jnp.zeros((WINDOW, width), bf16)
        vbuf[pad:base] = jnp.zeros((WINDOW, width), bf16)

    grads[...] = jnp.zeros_like(grads)
    for load in loads:
        load.wait()

    def halo_copy(which, s, size):
        buf = (kbuf, vbuf)[which]
        start = base + s * rows + rows - size
        return pltpu.make_async_remote_copy(
            src_ref=buf.at[pl.ds(pl.multiple_of(start, 16), size)],
            dst_ref=buf.at[pl.ds(pl.multiple_of(start - stretch, 16), size)],
            send_sem=halo_s.at[which, s], recv_sem=halo_r.at[which, s],
            device_id={"grp": grp + 1},
        )

    def for_halo(which, s, present, act):
        @pl.when(jnp.logical_and(present, s == halo_first))
        def _():
            act(halo_copy(which, s, halo_part))

        @pl.when(jnp.logical_and(present, s > halo_first))
        def _():
            act(halo_copy(which, s, rows))

    def rms_unit(x):
        x = x.astype(f32)
        return (x * lax.rsqrt(jnp.mean(x * x, axis=1, keepdims=True) + EPSILON)).astype(bf16)

    @pl.loop(0, members)
    def _(d):
        s = other_member(me, d, members)

        @pl.when(d == 0)
        def _():
            kept(k_hbm, kbuf, base, k_r).wait()

        @pl.when(d > 0)
        def _():
            exchange(k_hbm, kbuf, base, k_s, k_r, d).wait_recv()

        for_halo(0, s, has_upper, lambda copy: copy.start())

        @pl.when(d > 1)
        def _():
            exchange(v_hbm, vbuf, base, v_s, v_r, d).start()

        @pl.when(d == 0)
        def _():
            kept(v_hbm, vbuf, base, v_r).wait()

        @pl.when(d == 1)
        def _():
            exchange(v_hbm, vbuf, base, v_s, v_r, d).wait_recv()

        for_halo(1, s, jnp.logical_and(has_upper, d < 2), lambda copy: copy.start())

    @pl.loop(0, members)
    def _(d):
        here = own_rows(other_member(me, d, members))
        there = own_rows(other_member(me, d, members), 0)
        key_unit = rms_unit(kbuf[here])
        a = dot_nn(key_unit, weights[0])
        b = dot_nn(key_unit, weights[1])
        sig = 1.0 / (1.0 + jnp.exp(-a))
        active = a * sig
        units[there] = key_unit
        hiddens[there] = (active * b).astype(bf16)
        gates[there] = active
        slopes[there] = b * sig * (1.0 + a * (1.0 - sig))

    @pl.loop(0, members)
    def _(d):
        s = other_member(me, d, members)
        there = own_rows(s, 0)

        @pl.when(d == 0)
        def _():
            own_rates.wait()

        @pl.when(d > 0)
        def _():
            rates_to(d).wait_recv()

        @pl.when(d > 1)
        def _():
            exchange(v_hbm, vbuf, base, v_s, v_r, d).wait_recv()

        @pl.when(d > 0)
        def _():
            exchange(q_hbm, qbuf, 0, q_s, q_r, d).start()

        heads_rates = rbuf[s]
        is_mine = lax.broadcasted_iota(jnp.int32, heads_rates.shape, 0) == me
        rate_row = jnp.sum(jnp.where(is_mine, heads_rates, 0.0), axis=0, keepdims=True)
        diagonal = lax.broadcasted_iota(jnp.int32, (rows, rows), 0) == lax.broadcasted_iota(
            jnp.int32, (rows, rows), 1
        )
        rate = jnp.sum(jnp.where(diagonal, rate_row, 0.0), axis=1, keepdims=True)
        delta_out = (-rate * vbuf[own_rows(s)].astype(f32)).astype(bf16)
        dh = dot_nt(delta_out, weights[2])
        key_unit = units[there]
        delta_three = (dh * gates[there]).astype(bf16)
        delta_one = (dh * slopes[there]).astype(bf16)
        grads[0:width] += dot_tn(key_unit, delta_one)
        grads[width : 2 * width] += dot_tn(key_unit, delta_three)
        grads[2 * width : 3 * width] += dot_tn(hiddens[there], delta_out)

    def rows_of(i):
        return pl.ds(pl.multiple_of(i * chunk, chunk), chunk)

    def inward(i, target, recv):
        return pltpu.make_async_remote_copy(
            src_ref=to_inner.at[i], dst_ref=target.at[i],
            send_sem=inner_s.at[i], recv_sem=recv.at[i], device_id={"grp": inner},
        )

    def outward(i):
        return pltpu.make_async_remote_copy(
            src_ref=to_outer.at[i], dst_ref=from_inner.at[i],
            send_sem=outer_s.at[i], recv_sem=inner_r.at[i], device_id={"grp": outer},
        )

    def send_inward(i):
        @pl.when(is_mid)
        def _():
            inward(i, from_inner, inner_r).start()

        @pl.when(jnp.logical_not(is_mid))
        def _():
            inward(i, from_outer, outer_r).start()

    @pl.when(jnp.logical_not(has_outer))
    def _():
        @pl.loop(0, chunks)
        def _(i):
            to_inner[i] = grads[rows_of(i)].astype(bf16)
            send_inward(i)

    def attend(s):
        scores = dot_nt(qbuf[own_rows(s, 0)], kbuf[pl.ds(pl.multiple_of(s * rows, 16), reach)])
        scores = scores * width ** (-0.5)
        query = lax.broadcasted_iota(jnp.int32, (rows, reach), 0)
        key = lax.broadcasted_iota(jnp.int32, (rows, reach), 1)
        offset = query - key + base
        first = grp * stretch + s * rows - base
        allowed = (offset >= 0) & (offset < WINDOW) & (key + first >= 0)
        scores = jnp.where(allowed, scores, -1e30)
        top = jnp.max(scores, axis=1, keepdims=True)
        exponent = jnp.exp(scores - top)
        total = jnp.sum(exponent, axis=1, keepdims=True)
        out = dot_nn(
            exponent.astype(bf16), vbuf[pl.ds(pl.multiple_of(s * rows, 16), reach)]
        )
        return (out / total).astype(bf16)

    def orthogonal_update(m):
        gradient = grads[pl.ds(pl.multiple_of(m * width, width), width)]
        squares = jnp.sum(jnp.sum(gradient * gradient, axis=1, keepdims=True), axis=0, keepdims=True)
        current = (gradient / (jnp.sqrt(squares) + 1e-07)).astype(bf16)
        for sweep_index in range(NS_STEPS):
            gram = dot_nt(current, current).astype(bf16)
            mixer = (COEF_B * gram.astype(f32) + COEF_C * dot_nn(gram, gram)).astype(bf16)
            current = (COEF_A * current.astype(f32) + dot_nn(mixer, current)).astype(bf16)
        updated[m] = (weights[m].astype(f32) - current.astype(f32)).astype(bf16)

    def attend_and_send(s):
        piece = s + halo_first
        for which in range(2):
            for_halo(
                which, piece, jnp.logical_and(has_lower, piece < members),
                lambda copy: copy.wait_recv(),
            )
        window_send[s] = attend(s)

        @pl.when(s == me)
        def _():
            block_kept(window_send, window_recv, win_r).start()

        @pl.when(s != me)
        def _():
            block_to(window_send, window_recv, win_s, win_r, s).start()

    halo_step = jnp.where(grp == 0, chunks - 4, jnp.where(in_lower, chunks, chunks + 1))
    per_matrix = width // chunk
    lag = 2

    @pl.loop(0, chunks + lag)
    def _(i):
        @pl.when(jnp.logical_and(has_outer, i < chunks))
        def _():
            inward(i, from_outer, outer_r).wait_recv()
            partial = grads[rows_of(i)] + from_outer[i].astype(f32)
            to_inner[i] = partial.astype(bf16)
            send_inward(i)

        @pl.when(i >= lag)
        def _():
            j = i - lag
            outward(j).wait_recv()

            @pl.when(is_mid)
            def _():
                grads[rows_of(j)] = to_inner[j].astype(f32) + from_inner[j].astype(f32)

            @pl.when(jnp.logical_not(is_mid))
            def _():
                grads[rows_of(j)] = from_inner[j].astype(f32)

            @pl.when(has_outer)
            def _():
                to_outer[j] = grads[rows_of(j)].astype(bf16)
                outward(j).start()

            @pl.when(lax.rem(j, per_matrix) == per_matrix - 1)
            def _():
                orthogonal_update(j // per_matrix)

        @pl.when(i == halo_step)
        def _():
            @pl.loop(2, members)
            def _(d):
                for_halo(1, other_member(me, d, members), has_upper, lambda copy: copy.start())

        @pl.when(i == chunks - members)
        def _():
            kept(q_hbm, qbuf, 0, q_r).wait()

            @pl.loop(1, members)
            def _(d):
                exchange(q_hbm, qbuf, 0, q_s, q_r, d).wait_recv()

        late = chunks - 1 - i
        ready = jnp.logical_or(grp == 0, late + halo_first >= members)

        @pl.when((i >= chunks - members) & (i < chunks) & ready)
        def _():
            attend_and_send(late)

    gain = gain_ref[me]

    @pl.loop(0, members)
    def _(d):
        s = other_member(me, members - 1 - d, members)
        unit = rms_unit(qbuf[own_rows(s, 0)])
        a = dot_nn(unit, updated[0])
        b = dot_nn(unit, updated[1])
        hidden = (a / (1.0 + jnp.exp(-a)) * b).astype(bf16)
        fast_send[s] = (dot_nn(hidden, updated[2]) * gain).astype(bf16)

        @pl.when(s == me)
        def _():
            block_kept(fast_send, fast_recv, fast_r).start()

        @pl.when(s != me)
        def _():
            block_to(fast_send, fast_recv, fast_s, fast_r, s).start()

    @pl.when(has_lower)
    def _():
        @pl.loop(0, members - halo_first)
        def _(i):
            attend_and_send(members - halo_first - 1 - i)

    block_kept(window_send, window_recv, win_r).wait()
    block_kept(fast_send, fast_recv, fast_r).wait()

    @pl.loop(1, members)
    def _(d):
        s = other_member(me, d, members)
        block_to(window_send, window_recv, win_s, win_r, s).wait_recv()
        block_to(fast_send, fast_recv, fast_s, fast_r, s).wait_recv()

    @pl.loop(1, members)
    def _(d):
        s = other_member(me, d, members)
        rates_to(d).wait_send()
        exchange(k_hbm, kbuf, base, k_s, k_r, d).wait_send()
        exchange(v_hbm, vbuf, base, v_s, v_r, d).wait_send()
        exchange(q_hbm, qbuf, 0, q_s, q_r, d).wait_send()
        block_to(window_send, window_recv, win_s, win_r, s).wait_send()
        block_to(fast_send, fast_recv, fast_s, fast_r, s).wait_send()

    @pl.loop(0, members)
    def _(s):
        for which in range(2):
            for_halo(which, s, has_upper, lambda copy: copy.wait_send())

    @pl.loop(0, chunks)
    def _(i):
        inward(i, from_inner, inner_r).wait_send()

        @pl.when(has_outer)
        def _():
            outward(i).wait_send()


def norm_kernel(window_raw, fast_raw, window_ref, fast_ref):
    heads, _, width = window_raw.shape
    for raw, out in ((window_raw, window_ref), (fast_raw, fast_ref)):
        total = 0.0
        for h in range(heads):
            x = raw[h].astype(jnp.float32)
            total = total + jnp.sum(x * x, axis=1, keepdims=True)
        scale = lax.rsqrt(total / (heads * width) + EPSILON)
        for h in range(heads):
            out[:, h * width : (h + 1) * width] = (raw[h].astype(jnp.float32) * scale).astype(
                jnp.bfloat16
            )


def normed_rows(window_raw, fast_raw):
    heads, rows, width = window_raw.shape
    block = 64
    raw = pl.BlockSpec((heads, block, width), lambda i: (0, i, 0))
    done = pl.BlockSpec((block, heads * width), lambda i: (i, 0))
    out = jax.ShapeDtypeStruct((rows, heads * width), jnp.bfloat16)
    return pl.pallas_call(
        norm_kernel,
        grid=(rows // block,),
        out_shape=(out, out),
        in_specs=[raw, raw],
        out_specs=(done, done),
        compiler_params=pltpu.CompilerParams(vmem_limit_bytes=60 * 2**20),
        cost_estimate=pl.CostEstimate(
            flops=8 * rows * heads * width, bytes_accessed=8 * rows * heads * width, transcendentals=0
        ),
    )(window_raw, fast_raw)


def local_kernel(queries, key_rows, value_rows, token_rates, fast_one, fast_three, fast_two, head_gain):
    groups, members = lax.axis_size("grp"), lax.axis_size("mem")
    rows, width = queries.shape[0], fast_one.shape[1]
    pad = -(WINDOW + rows) % 128
    chunk = 128
    chunks = 3 * width // chunk
    bf16, dma = jnp.bfloat16, pltpu.SemaphoreType.DMA
    keys = pltpu.VMEM((pad + WINDOW + members * rows, width), bf16)
    tokens = pltpu.VMEM((members * rows, width), bf16)
    parts = pltpu.VMEM((chunks, chunk, width), bf16)
    blocks = pltpu.VMEM((members, rows, width), bf16)
    matrices = pltpu.VMEM((3, width, width), bf16)
    anywhere = pl.BlockSpec(memory_space=pl.ANY)
    out = jax.ShapeDtypeStruct((members, rows, width), bf16)
    window_raw, fast_raw = pl.pallas_call(
        functools.partial(layer_kernel, (groups, members, rows, width, pad, chunk)),
        out_shape=(out, out),
        in_specs=[anywhere] * 7 + [pl.BlockSpec(memory_space=pltpu.SMEM)],
        out_specs=(anywhere, anywhere),
        scratch_shapes=[
            keys, keys, tokens,
            pltpu.VMEM((members, members, rows), jnp.float32),
            matrices, matrices, pltpu.VMEM((3 * width, width), jnp.float32),
            parts, parts, parts, parts, blocks, blocks,
            tokens, tokens, pltpu.VMEM((members * rows, width), jnp.float32),
            pltpu.VMEM((members * rows, width), jnp.float32),
        ]
        + [dma((members,))] * 8
        + [dma((2, members))] * 2
        + [dma((chunks,))] * 4
        + [dma((members,))] * 4
        + [dma((3,))],
        compiler_params=pltpu.CompilerParams(
            collective_id=0, has_side_effects=True, vmem_limit_bytes=56 * 2**20
        ),
        cost_estimate=pl.CostEstimate(
            flops=16 * 2**30, bytes_accessed=10 * 2**20, transcendentals=4 * 2**20
        ),
    )(key_rows, value_rows, queries, token_rates.T, fast_one, fast_three, fast_two, head_gain)
    return normed_rows(window_raw, fast_raw)


def solution(mesh):
    ctx, head = mesh.shape["ctx"], mesh.shape["head"]
    def run(*args):
        members = args[4].shape[0] // head
        split = Mesh(mesh.devices.reshape(ctx // members, members, head), ("grp", "mem", "head"))
        rows = P(("grp", "mem"), "head")
        weights = P("head", None, None)
        groups, width, rows_here = ctx // members, args[4].shape[1], args[0].shape[0] // ctx
        whole_blocks = rows_here % 64 == 0 and width % 128 == 0 and members * rows_here > WINDOW
        pairs = groups % 2 == 0 and members > 1 and members & (members - 1) == 0
        fits = whole_blocks and pairs and members % 8 == 0 and 3 * width // 128 >= members
        return jax.shard_map(
            local_kernel if fits and head == 1 else local,
            mesh=split,
            in_specs=(rows, rows, rows, rows, weights, weights, weights, P("head")),
            out_specs=(rows, rows),
            check_vma=False,
        )(*args)

    return run
```

```python
import functools

import jax
import jax.numpy as jnp
from jax import lax
from jax.experimental import pallas as pl
from jax.experimental.pallas import tpu as pltpu
from jax.sharding import Mesh
from jax.sharding import PartitionSpec as P

WINDOW = 1024
NS_STEPS = 2

COEF_A = 3.4445
COEF_B = -4.775
COEF_C = 2.0315
EPSILON = 1e-06


def rms_heads(block):
    return block / jnp.sqrt(jnp.mean(block * block, axis=-1, keepdims=True) + EPSILON)


def to_heads(rows):
    return lax.all_to_all(rows, "mem", split_axis=1, concat_axis=0, tiled=True)


def to_tokens(rows):
    return lax.all_to_all(rows, "mem", split_axis=0, concat_axis=1, tiled=True)


def with_earlier(rows):
    tokens, groups = rows.shape[0], lax.axis_size("grp")
    parts, missing, distance = [rows], WINDOW, 1
    while missing > 0:
        take = min(missing, tokens)
        pairs = [(i, i + distance) for i in range(groups - distance)]
        parts.insert(0, lax.ppermute(rows[tokens - take :], "grp", pairs))
        missing -= take
        distance += 1
    return jnp.concatenate(parts, axis=0)


def window_attention(q, k, v):
    tokens, width = q.shape
    block = 512 if tokens % 512 == 0 else tokens
    count = tokens // block
    keys, values = with_earlier(k), with_earlier(v)
    reach = WINDOW + block
    keys = jnp.stack([keys[i * block : i * block + reach] for i in range(count)])
    values = jnp.stack([values[i * block : i * block + reach] for i in range(count)])
    scores = jnp.einsum(
        "bqd,bkd->bqk", q.reshape(count, block, width), keys, preferred_element_type=jnp.float32
    ) * width ** (-0.5)
    query_pos = lax.broadcasted_iota(jnp.int32, (count, block, reach), 1) + WINDOW
    key_pos = lax.broadcasted_iota(jnp.int32, (count, block, reach), 2)
    base = lax.broadcasted_iota(jnp.int32, (count, block, reach), 0) * block
    first_key = lax.axis_index("grp") * tokens - WINDOW
    offset = query_pos - key_pos
    allowed = (offset >= 0) & (offset < WINDOW) & (key_pos + base + first_key >= 0)
    scores = jnp.where(allowed, scores, -1e30)
    row_top = jnp.max(scores, axis=-1, keepdims=True)
    exponent = jnp.exp(scores - row_top)
    weights = (exponent / jnp.sum(exponent, axis=-1, keepdims=True)).astype(jnp.bfloat16)
    out = jnp.einsum("bqk,bkd->bqd", weights, values, preferred_element_type=jnp.float32)
    return out.reshape(tokens, width)


def orthogonal(gradient):
    squares = jnp.sum(gradient * gradient)
    current = (gradient / (jnp.sqrt(squares) + 1e-07)).astype(jnp.bfloat16)
    for sweep_index in range(NS_STEPS):
        gram = jnp.einsum(
            "rc,sc->rs", current, current, preferred_element_type=jnp.float32
        ).astype(jnp.bfloat16)
        mixer = (
            COEF_B * gram.astype(jnp.float32)
            + COEF_C * jnp.dot(gram, gram, preferred_element_type=jnp.float32)
        ).astype(jnp.bfloat16)
        current = (
            COEF_A * current.astype(jnp.float32)
            + jnp.dot(mixer, current, preferred_element_type=jnp.float32)
        ).astype(jnp.bfloat16)
    return current


def fast_weights(q, k, v, rates, one, three, two):
    f32 = jnp.float32
    key_normed = rms_heads(k.astype(f32)).astype(jnp.bfloat16)
    query_normed = rms_heads(q.astype(f32)).astype(jnp.bfloat16)
    hidden_one = jnp.dot(key_normed, one, preferred_element_type=f32)
    hidden_three = jnp.dot(key_normed, three, preferred_element_type=f32)
    sigmoid_one = jax.nn.sigmoid(hidden_one)
    active = hidden_one * sigmoid_one
    hidden = (active * hidden_three).astype(jnp.bfloat16)
    delta_out = (-rates * v.astype(f32)).astype(jnp.bfloat16)
    delta_hidden = jnp.einsum("td,fd->tf", delta_out, two, preferred_element_type=f32)
    delta_three = (delta_hidden * active).astype(jnp.bfloat16)
    delta_one = (
        delta_hidden * hidden_three * sigmoid_one * (1.0 + hidden_one * (1.0 - sigmoid_one))
    ).astype(jnp.bfloat16)
    gradient_one = jnp.einsum("td,tf->df", key_normed, delta_one, preferred_element_type=f32)
    gradient_three = jnp.einsum("td,tf->df", key_normed, delta_three, preferred_element_type=f32)
    gradient_two = jnp.einsum("tf,td->fd", hidden, delta_out, preferred_element_type=f32)
    grads = lax.psum(jnp.stack([gradient_one, gradient_three, gradient_two]), "grp")
    new = [
        (old.astype(f32) - orthogonal(grads[i]).astype(f32)).astype(jnp.bfloat16)
        for i, old in enumerate((one, three, two))
    ]
    query_one = jnp.dot(query_normed, new[0], preferred_element_type=f32)
    query_three = jnp.dot(query_normed, new[1], preferred_element_type=f32)
    query_hidden = (jax.nn.silu(query_one) * query_three).astype(jnp.bfloat16)
    return jnp.dot(query_hidden, new[2], preferred_element_type=f32)


def normed(rows):
    rows = rows.astype(jnp.float32)
    heads = lax.axis_size("head")
    total = lax.psum(jnp.sum(rows * rows, axis=1, keepdims=True), "head")
    return (rows / jnp.sqrt(total / (rows.shape[1] * heads) + EPSILON)).astype(jnp.bfloat16)


def local(queries, key_rows, value_rows, token_rates, fast_one, fast_three, fast_two, head_gain):
    me = lax.axis_index("mem")
    k, v, q = to_heads(key_rows), to_heads(value_rows), to_heads(queries)
    first = lax.axis_index("head") * head_gain.shape[0] if token_rates.shape[1] != head_gain.shape[0] else 0
    rates = lax.all_gather(token_rates, "mem", axis=0, tiled=True)
    rates = lax.dynamic_slice_in_dim(rates, me + first, 1, axis=1)
    one, three, two = (
        lax.dynamic_index_in_dim(w, me, 0, keepdims=False) for w in (fast_one, fast_three, fast_two)
    )
    gain = lax.dynamic_index_in_dim(head_gain, me, 0, keepdims=False)
    attended = window_attention(q, k, v)
    fast = fast_weights(q, k, v, rates, one, three, two) * gain
    window_rows = to_tokens(attended.astype(jnp.bfloat16))
    fast_rows = to_tokens(fast.astype(jnp.bfloat16))
    return normed(window_rows), normed(fast_rows)


def dot_nn(a, b):
    return jnp.dot(a, b, preferred_element_type=jnp.float32)


def dot_nt(a, b):
    return lax.dot_general(a, b, (((1,), (1,)), ((), ())), preferred_element_type=jnp.float32)


def dot_tn(a, b):
    return lax.dot_general(a, b, (((0,), (0,)), ((), ())), preferred_element_type=jnp.float32)


def other_member(a, b, count):
    out, bit = 0, 1
    while bit < count:
        out = out + bit * lax.rem(a // bit + b // bit, 2)
        bit *= 2
    return out


def layer_kernel(
    dims, k_hbm, v_hbm, q_hbm, rates_hbm, one_hbm, three_hbm, two_hbm, gain_ref,
    window_recv, fast_recv,
    kbuf, vbuf, qbuf, rbuf, weights, updated, grads, from_outer, from_inner, to_inner, to_outer,
    window_send, fast_send, units, hiddens, gates, slopes,
    k_s, k_r, v_s, v_r, q_s, q_r, r_s, r_r, halo_s, halo_r, outer_r, inner_r, inner_s, outer_s,
    win_s, win_r, fast_s, fast_r, load_sem,
):
    groups, members, rows, width, pad, chunk = dims
    f32, bf16 = jnp.float32, jnp.bfloat16
    me, grp = lax.axis_index("mem"), lax.axis_index("grp")
    base = pad + WINDOW
    reach = base + rows
    stretch = members * rows
    chunks = 3 * width // chunk
    halo_first = (stretch - WINDOW) // rows
    halo_part = (halo_first + 1) * rows - (stretch - WINDOW)
    has_lower, has_upper = grp > 0, grp < groups - 1
    has_outer = jnp.logical_and(has_lower, has_upper)
    in_lower = grp < groups // 2
    inner = jnp.where(in_lower, grp + 1, grp - 1)
    outer = jnp.where(in_lower, grp - 1, grp + 1)
    is_mid = jnp.logical_or(grp == groups // 2 - 1, grp == groups // 2)

    barrier = pltpu.get_barrier_semaphore()
    for d in range(1, members):
        pl.semaphore_signal(barrier, inc=1, device_id={"mem": lax.rem(me + d, members)})

    @pl.when(has_lower)
    def _():
        pl.semaphore_signal(barrier, inc=1, device_id={"grp": grp - 1})

    @pl.when(has_upper)
    def _():
        pl.semaphore_signal(barrier, inc=1, device_id={"grp": grp + 1})

    pl.semaphore_wait(
        barrier, members - 1 + jnp.minimum(grp, 1) + jnp.minimum(groups - 1 - grp, 1)
    )

    def cols(p):
        return pl.ds(pl.multiple_of(p * width, width), width)

    def own_rows(s, first=base):
        return pl.ds(pl.multiple_of(first + s * rows, 16), rows)

    def exchange(hbm, buf, first, send, recv, d):
        peer = other_member(me, d, members)
        return pltpu.make_async_remote_copy(
            src_ref=hbm.at[:, cols(peer)], dst_ref=buf.at[own_rows(me, first)],
            send_sem=send.at[d], recv_sem=recv.at[d], device_id={"mem": peer},
        )

    def kept(hbm, buf, first, recv):
        return pltpu.make_async_copy(
            hbm.at[:, cols(me)], buf.at[own_rows(me, first)], recv.at[0]
        )

    def rates_to(d):
        peer = other_member(me, d, members)
        return pltpu.make_async_remote_copy(
            src_ref=rates_hbm, dst_ref=rbuf.at[me],
            send_sem=r_s.at[d], recv_sem=r_r.at[d], device_id={"mem": peer},
        )

    def block_to(send_buf, recv_buf, send, recv, s):
        d = other_member(me, s, members)
        return pltpu.make_async_remote_copy(
            src_ref=send_buf.at[s], dst_ref=recv_buf.at[me],
            send_sem=send.at[d], recv_sem=recv.at[d], device_id={"mem": s},
        )

    def block_kept(send_buf, recv_buf, recv):
        return pltpu.make_async_copy(send_buf.at[me], recv_buf.at[me], recv.at[0])

    own_rates = pltpu.make_async_copy(rates_hbm, rbuf.at[me], r_r.at[0])
    own_rates.start()
    kept(k_hbm, kbuf, base, k_r).start()
    kept(v_hbm, vbuf, base, v_r).start()
    kept(q_hbm, qbuf, 0, q_r).start()

    parity = lax.rem(me, 2)

    def pair_of(d):
        return (
            exchange(k_hbm, kbuf, base, k_s, k_r, d),
            exchange(v_hbm, vbuf, base, v_s, v_r, d),
        )

    for copy in pair_of(1):
        copy.start()

    @pl.loop(1, members // 2)
    def _(j):
        for copy in pair_of(2 * j + parity):
            copy.start()

    @pl.loop(1, members)
    def _(d):
        rates_to(d).start()

    loads = [
        pltpu.make_async_copy(hbm.at[me], weights.at[i], load_sem.at[i])
        for i, hbm in enumerate((one_hbm, three_hbm, two_hbm))
    ]
    for load in loads:
        load.start()
    kbuf[0:pad] = jnp.zeros((pad, width), bf16)
    vbuf[0:pad] = jnp.zeros((pad, width), bf16)

    @pl.when(grp == 0)
    def _():
        kbuf[pad:base] = jnp.zeros((WINDOW, width), bf16)
        vbuf[pad:base] = jnp.zeros((WINDOW, width), bf16)

    grads[...] = jnp.zeros_like(grads)
    for load in loads:
        load.wait()

    def halo_copy(which, s, size):
        buf = (kbuf, vbuf)[which]
        start = base + s * rows + rows - size
        return pltpu.make_async_remote_copy(
            src_ref=buf.at[pl.ds(pl.multiple_of(start, 16), size)],
            dst_ref=buf.at[pl.ds(pl.multiple_of(start - stretch, 16), size)],
            send_sem=halo_s.at[which, s], recv_sem=halo_r.at[which, s],
            device_id={"grp": grp + 1},
        )

    def for_halo(which, s, present, act):
        @pl.when(jnp.logical_and(present, s == halo_first))
        def _():
            act(halo_copy(which, s, halo_part))

        @pl.when(jnp.logical_and(present, s > halo_first))
        def _():
            act(halo_copy(which, s, rows))

    def queries_to(side):
        @pl.loop(0, members // 2)
        def _(j):
            d = 2 * j + jnp.where(parity == side, 0, 1)

            @pl.when(d > 0)
            def _():
                exchange(q_hbm, qbuf, 0, q_s, q_r, d).start()

    def rms_unit(x):
        x = x.astype(f32)
        return (x * lax.rsqrt(jnp.mean(x * x, axis=1, keepdims=True) + EPSILON)).astype(bf16)

    kept(k_hbm, kbuf, base, k_r).wait()
    kept(v_hbm, vbuf, base, v_r).wait()
    for copy in pair_of(1):
        copy.wait_recv()
    for which in range(2):
        for d in range(2):
            for_halo(which, other_member(me, d, members), has_upper, lambda copy: copy.start())

    @pl.loop(1, members // 2)
    def _(j):
        for copy in pair_of(2 * j + parity):
            copy.wait_send()
        for copy in pair_of(2 * j + 1 - parity):
            copy.start()

    @pl.loop(0, members)
    def _(d):
        @pl.when(d > 1)
        def _():
            exchange(k_hbm, kbuf, base, k_s, k_r, d).wait_recv()

        here = own_rows(other_member(me, d, members))
        there = own_rows(other_member(me, d, members), 0)
        key_unit = rms_unit(kbuf[here])
        a = dot_nn(key_unit, weights[0])
        b = dot_nn(key_unit, weights[1])
        sig = 1.0 / (1.0 + jnp.exp(-a))
        active = a * sig
        units[there] = key_unit
        hiddens[there] = (active * b).astype(bf16)
        gates[there] = active
        slopes[there] = b * sig * (1.0 + a * (1.0 - sig))

    @pl.loop(0, members)
    def _(d):
        s = other_member(me, d, members)
        there = own_rows(s, 0)

        @pl.when(d == 0)
        def _():
            own_rates.wait()

        @pl.when(d > 0)
        def _():
            rates_to(d).wait_recv()

        @pl.when(d > 1)
        def _():
            exchange(v_hbm, vbuf, base, v_s, v_r, d).wait_recv()

        @pl.when((d == members // 2) & (parity == 1))
        def _():
            queries_to(0)

        heads_rates = rbuf[s]
        is_mine = lax.broadcasted_iota(jnp.int32, heads_rates.shape, 0) == me
        rate_row = jnp.sum(jnp.where(is_mine, heads_rates, 0.0), axis=0, keepdims=True)
        diagonal = lax.broadcasted_iota(jnp.int32, (rows, rows), 0) == lax.broadcasted_iota(
            jnp.int32, (rows, rows), 1
        )
        rate = jnp.sum(jnp.where(diagonal, rate_row, 0.0), axis=1, keepdims=True)
        delta_out = (-rate * vbuf[own_rows(s)].astype(f32)).astype(bf16)
        dh = dot_nt(delta_out, weights[2])
        key_unit = units[there]
        delta_three = (dh * gates[there]).astype(bf16)
        delta_one = (dh * slopes[there]).astype(bf16)
        grads[0:width] += dot_tn(key_unit, delta_one)
        grads[width : 2 * width] += dot_tn(key_unit, delta_three)
        grads[2 * width : 3 * width] += dot_tn(hiddens[there], delta_out)

    def rows_of(i):
        return pl.ds(pl.multiple_of(i * chunk, chunk), chunk)

    def inward(i, target, recv):
        return pltpu.make_async_remote_copy(
            src_ref=to_inner.at[i], dst_ref=target.at[i],
            send_sem=inner_s.at[i], recv_sem=recv.at[i], device_id={"grp": inner},
        )

    def outward(i):
        return pltpu.make_async_remote_copy(
            src_ref=to_outer.at[i], dst_ref=from_inner.at[i],
            send_sem=outer_s.at[i], recv_sem=inner_r.at[i], device_id={"grp": outer},
        )

    def send_inward(i):
        @pl.when(is_mid)
        def _():
            inward(i, from_inner, inner_r).start()

        @pl.when(jnp.logical_not(is_mid))
        def _():
            inward(i, from_outer, outer_r).start()

    @pl.when(jnp.logical_not(has_outer))
    def _():
        @pl.loop(0, chunks)
        def _(i):
            to_inner[i] = grads[rows_of(i)].astype(bf16)
            send_inward(i)

    def attend(s):
        scores = dot_nt(qbuf[own_rows(s, 0)], kbuf[pl.ds(pl.multiple_of(s * rows, 16), reach)])
        scores = scores * width ** (-0.5)
        query = lax.broadcasted_iota(jnp.int32, (rows, reach), 0)
        key = lax.broadcasted_iota(jnp.int32, (rows, reach), 1)
        offset = query - key + base
        first = grp * stretch + s * rows - base
        allowed = (offset >= 0) & (offset < WINDOW) & (key + first >= 0)
        scores = jnp.where(allowed, scores, -1e30)
        top = jnp.max(scores, axis=1, keepdims=True)
        exponent = jnp.exp(scores - top)
        total = jnp.sum(exponent, axis=1, keepdims=True)
        out = dot_nn(
            exponent.astype(bf16), vbuf[pl.ds(pl.multiple_of(s * rows, 16), reach)]
        )
        return (out / total).astype(bf16)

    def orthogonal_update(m):
        gradient = grads[pl.ds(pl.multiple_of(m * width, width), width)]
        squares = jnp.sum(jnp.sum(gradient * gradient, axis=1, keepdims=True), axis=0, keepdims=True)
        current = (gradient / (jnp.sqrt(squares) + 1e-07)).astype(bf16)
        for sweep_index in range(NS_STEPS):
            gram = dot_nt(current, current).astype(bf16)
            mixer = (COEF_B * gram.astype(f32) + COEF_C * dot_nn(gram, gram)).astype(bf16)
            current = (COEF_A * current.astype(f32) + dot_nn(mixer, current)).astype(bf16)
        updated[m] = (weights[m].astype(f32) - current.astype(f32)).astype(bf16)

    def attend_and_send(s):
        piece = s + halo_first
        for which in range(2):
            for_halo(
                which, piece, jnp.logical_and(has_lower, piece < members),
                lambda copy: copy.wait_recv(),
            )
        window_send[s] = attend(s)

        @pl.when(s == me)
        def _():
            block_kept(window_send, window_recv, win_r).start()

        @pl.when(s != me)
        def _():
            block_to(window_send, window_recv, win_s, win_r, s).start()

    halo_step = jnp.where(grp == 0, chunks - 4, jnp.where(in_lower, chunks, chunks + 1))
    per_matrix = width // chunk
    @pl.when(parity == 1)
    def _():
        queries_to(1)

    lag = 2

    @pl.loop(0, chunks + lag)
    def _(i):
        @pl.when(jnp.logical_and(has_outer, i < chunks))
        def _():
            inward(i, from_outer, outer_r).wait_recv()
            partial = grads[rows_of(i)] + from_outer[i].astype(f32)
            to_inner[i] = partial.astype(bf16)
            send_inward(i)

        @pl.when(i >= lag)
        def _():
            j = i - lag
            outward(j).wait_recv()

            @pl.when(is_mid)
            def _():
                grads[rows_of(j)] = to_inner[j].astype(f32) + from_inner[j].astype(f32)

            @pl.when(jnp.logical_not(is_mid))
            def _():
                grads[rows_of(j)] = from_inner[j].astype(f32)

            @pl.when(has_outer)
            def _():
                to_outer[j] = grads[rows_of(j)].astype(bf16)
                outward(j).start()

            @pl.when(lax.rem(j, per_matrix) == per_matrix - 1)
            def _():
                orthogonal_update(j // per_matrix)

        @pl.when(i == halo_step)
        def _():
            @pl.loop(2, members)
            def _(d):
                for which in range(2):
                    for_halo(
                        which, other_member(me, d, members), has_upper, lambda copy: copy.start()
                    )

        @pl.when((i == chunks - 4) & (parity == 0))
        def _():
            queries_to(0)

        @pl.when((i == chunks) & (parity == 0))
        def _():
            queries_to(1)

    kept(q_hbm, qbuf, 0, q_r).wait()

    @pl.loop(1, members)
    def _(d):
        exchange(q_hbm, qbuf, 0, q_s, q_r, d).wait_recv()

    gain = gain_ref[me]

    @pl.loop(0, members)
    def _(d):
        s = other_member(me, members - 1 - d, members)
        unit = rms_unit(qbuf[own_rows(s, 0)])
        a = dot_nn(unit, updated[0])
        b = dot_nn(unit, updated[1])
        hidden = (a / (1.0 + jnp.exp(-a)) * b).astype(bf16)
        fast_send[s] = (dot_nn(hidden, updated[2]) * gain).astype(bf16)

        @pl.when(s == me)
        def _():
            block_kept(fast_send, fast_recv, fast_r).start()

        @pl.when(s != me)
        def _():
            block_to(fast_send, fast_recv, fast_s, fast_r, s).start()

    @pl.loop(0, members)
    def _(i):
        attend_and_send(members - 1 - i)

    block_kept(window_send, window_recv, win_r).wait()
    block_kept(fast_send, fast_recv, fast_r).wait()

    @pl.loop(1, members)
    def _(d):
        s = other_member(me, d, members)
        block_to(window_send, window_recv, win_s, win_r, s).wait_recv()
        block_to(fast_send, fast_recv, fast_s, fast_r, s).wait_recv()

    @pl.loop(1, members)
    def _(d):
        s = other_member(me, d, members)
        rates_to(d).wait_send()

        @pl.when((d == 1) | (lax.rem(d, 2) != parity))
        def _():
            for copy in pair_of(d):
                copy.wait_send()

        exchange(q_hbm, qbuf, 0, q_s, q_r, d).wait_send()
        block_to(window_send, window_recv, win_s, win_r, s).wait_send()
        block_to(fast_send, fast_recv, fast_s, fast_r, s).wait_send()

    @pl.loop(0, members)
    def _(s):
        for which in range(2):
            for_halo(which, s, has_upper, lambda copy: copy.wait_send())

    @pl.loop(0, chunks)
    def _(i):
        inward(i, from_inner, inner_r).wait_send()

        @pl.when(has_outer)
        def _():
            outward(i).wait_send()


def norm_kernel(window_raw, fast_raw, window_ref, fast_ref):
    heads, _, width = window_raw.shape
    for raw, out in ((window_raw, window_ref), (fast_raw, fast_ref)):
        total = 0.0
        for h in range(heads):
            x = raw[h].astype(jnp.float32)
            total = total + jnp.sum(x * x, axis=1, keepdims=True)
        scale = lax.rsqrt(total / (heads * width) + EPSILON)
        for h in range(heads):
            out[:, h * width : (h + 1) * width] = (raw[h].astype(jnp.float32) * scale).astype(
                jnp.bfloat16
            )


def normed_rows(window_raw, fast_raw):
    heads, rows, width = window_raw.shape
    block = 64
    raw = pl.BlockSpec((heads, block, width), lambda i: (0, i, 0))
    done = pl.BlockSpec((block, heads * width), lambda i: (i, 0))
    out = jax.ShapeDtypeStruct((rows, heads * width), jnp.bfloat16)
    return pl.pallas_call(
        norm_kernel,
        grid=(rows // block,),
        out_shape=(out, out),
        in_specs=[raw, raw],
        out_specs=(done, done),
        compiler_params=pltpu.CompilerParams(vmem_limit_bytes=60 * 2**20),
        cost_estimate=pl.CostEstimate(
            flops=8 * rows * heads * width, bytes_accessed=8 * rows * heads * width, transcendentals=0
        ),
    )(window_raw, fast_raw)


def local_kernel(queries, key_rows, value_rows, token_rates, fast_one, fast_three, fast_two, head_gain):
    groups, members = lax.axis_size("grp"), lax.axis_size("mem")
    rows, width = queries.shape[0], fast_one.shape[1]
    pad = -(WINDOW + rows) % 128
    chunk = 128
    chunks = 3 * width // chunk
    bf16, dma = jnp.bfloat16, pltpu.SemaphoreType.DMA
    keys = pltpu.VMEM((pad + WINDOW + members * rows, width), bf16)
    tokens = pltpu.VMEM((members * rows, width), bf16)
    parts = pltpu.VMEM((chunks, chunk, width), bf16)
    blocks = pltpu.VMEM((members, rows, width), bf16)
    matrices = pltpu.VMEM((3, width, width), bf16)
    anywhere = pl.BlockSpec(memory_space=pl.ANY)
    out = jax.ShapeDtypeStruct((members, rows, width), bf16)
    window_raw, fast_raw = pl.pallas_call(
        functools.partial(layer_kernel, (groups, members, rows, width, pad, chunk)),
        out_shape=(out, out),
        in_specs=[anywhere] * 7 + [pl.BlockSpec(memory_space=pltpu.SMEM)],
        out_specs=(anywhere, anywhere),
        scratch_shapes=[
            keys, keys, tokens,
            pltpu.VMEM((members, members, rows), jnp.float32),
            matrices, matrices, pltpu.VMEM((3 * width, width), jnp.float32),
            parts, parts, parts, parts, blocks, blocks,
            tokens, tokens, pltpu.VMEM((members * rows, width), jnp.float32),
            pltpu.VMEM((members * rows, width), jnp.float32),
        ]
        + [dma((members,))] * 8
        + [dma((2, members))] * 2
        + [dma((chunks,))] * 4
        + [dma((members,))] * 4
        + [dma((3,))],
        compiler_params=pltpu.CompilerParams(
            collective_id=0, has_side_effects=True, vmem_limit_bytes=56 * 2**20
        ),
        cost_estimate=pl.CostEstimate(
            flops=16 * 2**30, bytes_accessed=10 * 2**20, transcendentals=4 * 2**20
        ),
    )(key_rows, value_rows, queries, token_rates.T, fast_one, fast_three, fast_two, head_gain)
    return normed_rows(window_raw, fast_raw)


def solution(mesh):
    ctx, head = mesh.shape["ctx"], mesh.shape["head"]
    def run(*args):
        members = args[4].shape[0] // head
        split = Mesh(mesh.devices.reshape(ctx // members, members, head), ("grp", "mem", "head"))
        rows = P(("grp", "mem"), "head")
        weights = P("head", None, None)
        groups, width, rows_here = ctx // members, args[4].shape[1], args[0].shape[0] // ctx
        whole_blocks = rows_here % 64 == 0 and width % 128 == 0 and members * rows_here > WINDOW
        pairs = groups % 2 == 0 and members > 1 and members & (members - 1) == 0
        fits = whole_blocks and pairs and members % 8 == 0 and 3 * width // 128 >= members
        return jax.shard_map(
            local_kernel if fits and head == 1 else local,
            mesh=split,
            in_specs=(rows, rows, rows, rows, weights, weights, weights, P("head")),
            out_specs=(rows, rows),
            check_vma=False,
        )(*args)

    return run
```

```python
import functools

import jax
import jax.numpy as jnp
from jax import lax
from jax.experimental import pallas as pl
from jax.experimental.pallas import tpu as pltpu
from jax.sharding import Mesh
from jax.sharding import PartitionSpec as P

WINDOW = 1024
NS_STEPS = 2

COEF_A = 3.4445
COEF_B = -4.775
COEF_C = 2.0315
EPSILON = 1e-06


def rms_heads(block):
    return block / jnp.sqrt(jnp.mean(block * block, axis=-1, keepdims=True) + EPSILON)


def to_heads(rows):
    return lax.all_to_all(rows, "mem", split_axis=1, concat_axis=0, tiled=True)


def to_tokens(rows):
    return lax.all_to_all(rows, "mem", split_axis=0, concat_axis=1, tiled=True)


def with_earlier(rows):
    tokens, groups = rows.shape[0], lax.axis_size("grp")
    parts, missing, distance = [rows], WINDOW, 1
    while missing > 0:
        take = min(missing, tokens)
        pairs = [(i, i + distance) for i in range(groups - distance)]
        parts.insert(0, lax.ppermute(rows[tokens - take :], "grp", pairs))
        missing -= take
        distance += 1
    return jnp.concatenate(parts, axis=0)


def window_attention(q, k, v):
    tokens, width = q.shape
    block = 512 if tokens % 512 == 0 else tokens
    count = tokens // block
    keys, values = with_earlier(k), with_earlier(v)
    reach = WINDOW + block
    keys = jnp.stack([keys[i * block : i * block + reach] for i in range(count)])
    values = jnp.stack([values[i * block : i * block + reach] for i in range(count)])
    scores = jnp.einsum(
        "bqd,bkd->bqk", q.reshape(count, block, width), keys, preferred_element_type=jnp.float32
    ) * width ** (-0.5)
    query_pos = lax.broadcasted_iota(jnp.int32, (count, block, reach), 1) + WINDOW
    key_pos = lax.broadcasted_iota(jnp.int32, (count, block, reach), 2)
    base = lax.broadcasted_iota(jnp.int32, (count, block, reach), 0) * block
    first_key = lax.axis_index("grp") * tokens - WINDOW
    offset = query_pos - key_pos
    allowed = (offset >= 0) & (offset < WINDOW) & (key_pos + base + first_key >= 0)
    scores = jnp.where(allowed, scores, -1e30)
    row_top = jnp.max(scores, axis=-1, keepdims=True)
    exponent = jnp.exp(scores - row_top)
    weights = (exponent / jnp.sum(exponent, axis=-1, keepdims=True)).astype(jnp.bfloat16)
    out = jnp.einsum("bqk,bkd->bqd", weights, values, preferred_element_type=jnp.float32)
    return out.reshape(tokens, width)


def orthogonal(gradient):
    squares = jnp.sum(gradient * gradient)
    current = (gradient / (jnp.sqrt(squares) + 1e-07)).astype(jnp.bfloat16)
    for sweep_index in range(NS_STEPS):
        gram = jnp.einsum(
            "rc,sc->rs", current, current, preferred_element_type=jnp.float32
        ).astype(jnp.bfloat16)
        mixer = (
            COEF_B * gram.astype(jnp.float32)
            + COEF_C * jnp.dot(gram, gram, preferred_element_type=jnp.float32)
        ).astype(jnp.bfloat16)
        current = (
            COEF_A * current.astype(jnp.float32)
            + jnp.dot(mixer, current, preferred_element_type=jnp.float32)
        ).astype(jnp.bfloat16)
    return current


def fast_weights(q, k, v, rates, one, three, two):
    f32 = jnp.float32
    key_normed = rms_heads(k.astype(f32)).astype(jnp.bfloat16)
    query_normed = rms_heads(q.astype(f32)).astype(jnp.bfloat16)
    hidden_one = jnp.dot(key_normed, one, preferred_element_type=f32)
    hidden_three = jnp.dot(key_normed, three, preferred_element_type=f32)
    sigmoid_one = jax.nn.sigmoid(hidden_one)
    active = hidden_one * sigmoid_one
    hidden = (active * hidden_three).astype(jnp.bfloat16)
    delta_out = (-rates * v.astype(f32)).astype(jnp.bfloat16)
    delta_hidden = jnp.einsum("td,fd->tf", delta_out, two, preferred_element_type=f32)
    delta_three = (delta_hidden * active).astype(jnp.bfloat16)
    delta_one = (
        delta_hidden * hidden_three * sigmoid_one * (1.0 + hidden_one * (1.0 - sigmoid_one))
    ).astype(jnp.bfloat16)
    gradient_one = jnp.einsum("td,tf->df", key_normed, delta_one, preferred_element_type=f32)
    gradient_three = jnp.einsum("td,tf->df", key_normed, delta_three, preferred_element_type=f32)
    gradient_two = jnp.einsum("tf,td->fd", hidden, delta_out, preferred_element_type=f32)
    grads = lax.psum(jnp.stack([gradient_one, gradient_three, gradient_two]), "grp")
    new = [
        (old.astype(f32) - orthogonal(grads[i]).astype(f32)).astype(jnp.bfloat16)
        for i, old in enumerate((one, three, two))
    ]
    query_one = jnp.dot(query_normed, new[0], preferred_element_type=f32)
    query_three = jnp.dot(query_normed, new[1], preferred_element_type=f32)
    query_hidden = (jax.nn.silu(query_one) * query_three).astype(jnp.bfloat16)
    return jnp.dot(query_hidden, new[2], preferred_element_type=f32)


def normed(rows):
    rows = rows.astype(jnp.float32)
    heads = lax.axis_size("head")
    total = lax.psum(jnp.sum(rows * rows, axis=1, keepdims=True), "head")
    return (rows / jnp.sqrt(total / (rows.shape[1] * heads) + EPSILON)).astype(jnp.bfloat16)


def local(queries, key_rows, value_rows, token_rates, fast_one, fast_three, fast_two, head_gain):
    me = lax.axis_index("mem")
    k, v, q = to_heads(key_rows), to_heads(value_rows), to_heads(queries)
    first = lax.axis_index("head") * head_gain.shape[0] if token_rates.shape[1] != head_gain.shape[0] else 0
    rates = lax.all_gather(token_rates, "mem", axis=0, tiled=True)
    rates = lax.dynamic_slice_in_dim(rates, me + first, 1, axis=1)
    one, three, two = (
        lax.dynamic_index_in_dim(w, me, 0, keepdims=False) for w in (fast_one, fast_three, fast_two)
    )
    gain = lax.dynamic_index_in_dim(head_gain, me, 0, keepdims=False)
    attended = window_attention(q, k, v)
    fast = fast_weights(q, k, v, rates, one, three, two) * gain
    window_rows = to_tokens(attended.astype(jnp.bfloat16))
    fast_rows = to_tokens(fast.astype(jnp.bfloat16))
    return normed(window_rows), normed(fast_rows)


def dot_nn(a, b):
    return jnp.dot(a, b, preferred_element_type=jnp.float32)


def dot_nt(a, b):
    return lax.dot_general(a, b, (((1,), (1,)), ((), ())), preferred_element_type=jnp.float32)


def dot_tn(a, b):
    return lax.dot_general(a, b, (((0,), (0,)), ((), ())), preferred_element_type=jnp.float32)


def other_member(a, b, count):
    out, bit = 0, 1
    while bit < count:
        out = out + bit * lax.rem(a // bit + b // bit, 2)
        bit *= 2
    return out


def layer_kernel(
    dims, k_hbm, v_hbm, q_hbm, rates_hbm, one_hbm, three_hbm, two_hbm, gain_ref,
    window_recv, fast_recv,
    kbuf, vbuf, qbuf, rbuf, weights, updated, grads, from_outer, from_inner, to_inner, to_outer,
    window_send, fast_send, units, hiddens, gates, slopes,
    from_upper, part_send, part_recv, stat_send, stat_recv,
    k_s, k_r, v_s, v_r, q_s, q_r, r_s, r_r, halo_s, halo_r, outer_r, inner_r, inner_s, outer_s,
    win_s, win_r, fast_s, fast_r, load_sem,
):
    groups, members, rows, width, pad, chunk = dims
    f32, bf16 = jnp.float32, jnp.bfloat16
    me, grp = lax.axis_index("mem"), lax.axis_index("grp")
    base = pad + WINDOW
    reach = base + rows
    stretch = members * rows
    chunks = 3 * width // chunk
    reaching = -(-WINDOW // rows)
    has_lower, has_upper = grp > 0, grp < groups - 1
    has_outer = jnp.logical_and(has_lower, has_upper)
    in_lower = grp < groups // 2
    inner = jnp.where(in_lower, grp + 1, grp - 1)
    outer = jnp.where(in_lower, grp - 1, grp + 1)
    is_mid = jnp.logical_or(grp == groups // 2 - 1, grp == groups // 2)

    barrier = pltpu.get_barrier_semaphore()
    for d in range(1, members):
        pl.semaphore_signal(barrier, inc=1, device_id={"mem": lax.rem(me + d, members)})

    @pl.when(has_lower)
    def _():
        pl.semaphore_signal(barrier, inc=1, device_id={"grp": grp - 1})

    @pl.when(has_upper)
    def _():
        pl.semaphore_signal(barrier, inc=1, device_id={"grp": grp + 1})

    pl.semaphore_wait(
        barrier, members - 1 + jnp.minimum(grp, 1) + jnp.minimum(groups - 1 - grp, 1)
    )

    def cols(p):
        return pl.ds(pl.multiple_of(p * width, width), width)

    def own_rows(s, first=base):
        return pl.ds(pl.multiple_of(first + s * rows, 16), rows)

    def exchange(hbm, buf, first, send, recv, d):
        peer = other_member(me, d, members)
        return pltpu.make_async_remote_copy(
            src_ref=hbm.at[:, cols(peer)], dst_ref=buf.at[own_rows(me, first)],
            send_sem=send.at[d], recv_sem=recv.at[d], device_id={"mem": peer},
        )

    def kept(hbm, buf, first, recv):
        return pltpu.make_async_copy(
            hbm.at[:, cols(me)], buf.at[own_rows(me, first)], recv.at[0]
        )

    def rates_to(d):
        peer = other_member(me, d, members)
        return pltpu.make_async_remote_copy(
            src_ref=rates_hbm, dst_ref=rbuf.at[me],
            send_sem=r_s.at[d], recv_sem=r_r.at[d], device_id={"mem": peer},
        )

    def block_to(send_buf, recv_buf, send, recv, s):
        d = other_member(me, s, members)
        return pltpu.make_async_remote_copy(
            src_ref=send_buf.at[s], dst_ref=recv_buf.at[me],
            send_sem=send.at[d], recv_sem=recv.at[d], device_id={"mem": s},
        )

    def block_kept(send_buf, recv_buf, recv):
        return pltpu.make_async_copy(send_buf.at[me], recv_buf.at[me], recv.at[0])

    own_rates = pltpu.make_async_copy(rates_hbm, rbuf.at[me], r_r.at[0])
    own_rates.start()
    kept(k_hbm, kbuf, base, k_r).start()
    kept(v_hbm, vbuf, base, v_r).start()
    kept(q_hbm, qbuf, 0, q_r).start()

    parity = lax.rem(me, 2)

    def pair_of(d):
        return (
            exchange(k_hbm, kbuf, base, k_s, k_r, d),
            exchange(v_hbm, vbuf, base, v_s, v_r, d),
        )

    for copy in pair_of(1):
        copy.start()

    @pl.loop(1, members // 2)
    def _(j):
        for copy in pair_of(2 * j + parity):
            copy.start()

    @pl.loop(1, members)
    def _(d):
        rates_to(d).start()

    loads = [
        pltpu.make_async_copy(hbm.at[me], weights.at[i], load_sem.at[i])
        for i, hbm in enumerate((one_hbm, three_hbm, two_hbm))
    ]
    for load in loads:
        load.start()
    kbuf[0:base] = jnp.zeros((base, width), bf16)
    vbuf[0:base] = jnp.zeros((base, width), bf16)
    grads[...] = jnp.zeros_like(grads)
    for load in loads:
        load.wait()

    def reach_copy(which, src, dst, s, target):
        return pltpu.make_async_remote_copy(
            src_ref=src, dst_ref=dst.at[s],
            send_sem=halo_s.at[which, s], recv_sem=halo_r.at[which, s], device_id={"grp": target},
        )

    def query_down(s):
        return reach_copy(0, qbuf.at[own_rows(s, 0)], from_upper, s, grp - 1)

    def part_up(s):
        return (
            reach_copy(1, part_send.at[s], part_recv, s, grp + 1),
            reach_copy(2, stat_send.at[s], stat_recv, s, grp + 1),
        )

    def on_diagonal(values):
        diagonal = lax.broadcasted_iota(jnp.int32, (rows, rows), 0) == lax.broadcasted_iota(
            jnp.int32, (rows, rows), 1
        )
        return jnp.where(diagonal, values, 0.0)

    def as_column(row):
        return jnp.sum(on_diagonal(row), axis=1, keepdims=True)

    def as_row(column):
        return jnp.sum(on_diagonal(column), axis=0, keepdims=True)

    def queries_to(side):
        @pl.loop(0, members // 2)
        def _(j):
            d = 2 * j + jnp.where(parity == side, 0, 1)

            @pl.when(d > 0)
            def _():
                exchange(q_hbm, qbuf, 0, q_s, q_r, d).start()

    def rms_unit(x):
        x = x.astype(f32)
        return (x * lax.rsqrt(jnp.mean(x * x, axis=1, keepdims=True) + EPSILON)).astype(bf16)

    kept(k_hbm, kbuf, base, k_r).wait()
    kept(v_hbm, vbuf, base, v_r).wait()
    for copy in pair_of(1):
        copy.wait_recv()
    @pl.loop(1, members // 2)
    def _(j):
        for copy in pair_of(2 * j + parity):
            copy.wait_send()
        for copy in pair_of(2 * j + 1 - parity):
            copy.start()

    @pl.loop(0, members)
    def _(d):
        @pl.when(d > 1)
        def _():
            exchange(k_hbm, kbuf, base, k_s, k_r, d).wait_recv()

        here = own_rows(other_member(me, d, members))
        there = own_rows(other_member(me, d, members), 0)
        key_unit = rms_unit(kbuf[here])
        a = dot_nn(key_unit, weights[0])
        b = dot_nn(key_unit, weights[1])
        sig = 1.0 / (1.0 + jnp.exp(-a))
        active = a * sig
        units[there] = key_unit
        hiddens[there] = (active * b).astype(bf16)
        gates[there] = active
        slopes[there] = b * sig * (1.0 + a * (1.0 - sig))

    @pl.loop(0, members)
    def _(d):
        s = other_member(me, d, members)
        there = own_rows(s, 0)

        @pl.when(d == 0)
        def _():
            own_rates.wait()

        @pl.when(d > 0)
        def _():
            rates_to(d).wait_recv()

        @pl.when(d > 1)
        def _():
            exchange(v_hbm, vbuf, base, v_s, v_r, d).wait_recv()

        @pl.when((d == members // 2) & (parity == 1))
        def _():
            queries_to(0)

        heads_rates = rbuf[s]
        is_mine = lax.broadcasted_iota(jnp.int32, heads_rates.shape, 0) == me
        rate_row = jnp.sum(jnp.where(is_mine, heads_rates, 0.0), axis=0, keepdims=True)
        rate = as_column(rate_row)
        delta_out = (-rate * vbuf[own_rows(s)].astype(f32)).astype(bf16)
        dh = dot_nt(delta_out, weights[2])
        key_unit = units[there]
        delta_three = (dh * gates[there]).astype(bf16)
        delta_one = (dh * slopes[there]).astype(bf16)
        grads[0:width] += dot_tn(key_unit, delta_one)
        grads[width : 2 * width] += dot_tn(key_unit, delta_three)
        grads[2 * width : 3 * width] += dot_tn(hiddens[there], delta_out)

    def rows_of(i):
        return pl.ds(pl.multiple_of(i * chunk, chunk), chunk)

    def inward(i, target, recv):
        return pltpu.make_async_remote_copy(
            src_ref=to_inner.at[i], dst_ref=target.at[i],
            send_sem=inner_s.at[i], recv_sem=recv.at[i], device_id={"grp": inner},
        )

    def outward(i):
        return pltpu.make_async_remote_copy(
            src_ref=to_outer.at[i], dst_ref=from_inner.at[i],
            send_sem=outer_s.at[i], recv_sem=inner_r.at[i], device_id={"grp": outer},
        )

    def send_inward(i):
        @pl.when(is_mid)
        def _():
            inward(i, from_inner, inner_r).start()

        @pl.when(jnp.logical_not(is_mid))
        def _():
            inward(i, from_outer, outer_r).start()

    @pl.when(jnp.logical_not(has_outer))
    def _():
        @pl.loop(0, chunks)
        def _(i):
            to_inner[i] = grads[rows_of(i)].astype(bf16)
            send_inward(i)

    def softmax_parts(scores, values):
        top = jnp.max(scores, axis=1, keepdims=True)
        exponent = jnp.exp(scores - top)
        total = jnp.sum(exponent, axis=1, keepdims=True)
        return dot_nn(exponent.astype(bf16), values), top, total

    def attend(s):
        span = pl.ds(pl.multiple_of(s * rows, 16), reach)
        scores = dot_nt(qbuf[own_rows(s, 0)], kbuf[span]) * width ** (-0.5)
        query = lax.broadcasted_iota(jnp.int32, (rows, reach), 0)
        key = lax.broadcasted_iota(jnp.int32, (rows, reach), 1)
        offset = query - key + base
        allowed = (offset >= 0) & (offset < WINDOW) & (key + s * rows >= base)
        return softmax_parts(jnp.where(allowed, scores, -1e30), vbuf[span])

    def attend_for_upper(s):
        query_down(s).wait_recv()
        span = pl.ds(base + stretch - WINDOW, WINDOW)
        scores = dot_nt(from_upper[s], kbuf[span]) * width ** (-0.5)
        query = lax.broadcasted_iota(jnp.int32, (rows, WINDOW), 0)
        key = lax.broadcasted_iota(jnp.int32, (rows, WINDOW), 1)
        scores = jnp.where(query + s * rows < key, scores, -1e30)
        out, top, total = softmax_parts(scores, vbuf[span])
        part_send[s] = (out / total).astype(bf16)
        first = lax.broadcasted_iota(jnp.int32, (8, rows), 0) == 0
        stat_send[s] = jnp.where(first, as_row(top), as_row(total))
        for copy in part_up(s):
            copy.start()

    def orthogonal_update(m):
        gradient = grads[pl.ds(pl.multiple_of(m * width, width), width)]
        squares = jnp.sum(jnp.sum(gradient * gradient, axis=1, keepdims=True), axis=0, keepdims=True)
        current = (gradient / (jnp.sqrt(squares) + 1e-07)).astype(bf16)
        for sweep_index in range(NS_STEPS):
            gram = dot_nt(current, current).astype(bf16)
            mixer = (COEF_B * gram.astype(f32) + COEF_C * dot_nn(gram, gram)).astype(bf16)
            current = (COEF_A * current.astype(f32) + dot_nn(mixer, current)).astype(bf16)
        updated[m] = (weights[m].astype(f32) - current.astype(f32)).astype(bf16)

    def attend_and_send(s):
        out, top, total = attend(s)
        window_send[s] = (out / total).astype(bf16)

        @pl.when(has_lower & (s < reaching))
        def _():
            for copy in part_up(s):
                copy.wait_recv()
            stats = stat_recv[s]
            part_top, part_total = as_column(stats[0:1]), as_column(stats[1:2])
            whole_top = jnp.maximum(top, part_top)
            own_scale = jnp.exp(top - whole_top)
            part_scale = part_total * jnp.exp(part_top - whole_top)
            merged = out * own_scale + part_recv[s].astype(f32) * part_scale
            window_send[s] = (merged / (total * own_scale + part_scale)).astype(bf16)

        @pl.when(s == me)
        def _():
            block_kept(window_send, window_recv, win_r).start()

        @pl.when(s != me)
        def _():
            block_to(window_send, window_recv, win_s, win_r, s).start()

    def queries_here():
        kept(q_hbm, qbuf, 0, q_r).wait()

        @pl.loop(1, members)
        def _(d):
            exchange(q_hbm, qbuf, 0, q_s, q_r, d).wait_recv()

        @pl.when(has_lower)
        def _():
            @pl.loop(0, reaching)
            def _(i):
                query_down(reaching - 1 - i).start()

    per_matrix = width // chunk
    @pl.when(parity == 1)
    def _():
        queries_to(1)

    lag = 2

    @pl.loop(0, chunks + lag)
    def _(i):
        @pl.when(jnp.logical_and(has_outer, i < chunks))
        def _():
            inward(i, from_outer, outer_r).wait_recv()
            partial = grads[rows_of(i)] + from_outer[i].astype(f32)
            to_inner[i] = partial.astype(bf16)
            send_inward(i)

        @pl.when(i >= lag)
        def _():
            j = i - lag
            outward(j).wait_recv()

            @pl.when(is_mid)
            def _():
                grads[rows_of(j)] = to_inner[j].astype(f32) + from_inner[j].astype(f32)

            @pl.when(jnp.logical_not(is_mid))
            def _():
                grads[rows_of(j)] = from_inner[j].astype(f32)

            @pl.when(has_outer)
            def _():
                to_outer[j] = grads[rows_of(j)].astype(bf16)
                outward(j).start()

            @pl.when(lax.rem(j, per_matrix) == per_matrix - 1)
            def _():
                orthogonal_update(j // per_matrix)

        @pl.when((i == chunks - 4) & (parity == 0))
        def _():
            queries_to(0)

        @pl.when((i == chunks) & (parity == 0))
        def _():
            queries_to(1)

        first = chunks + lag - reaching - 1

        @pl.when((i == first - 1) & (parity == 1))
        def _():
            queries_here()

        @pl.when((i >= first) & (i < first + reaching) & (parity == 1) & has_upper)
        def _():
            attend_for_upper(reaching - 1 - (i - first))

    @pl.when(parity == 0)
    def _():
        queries_here()

    gain = gain_ref[me]

    @pl.loop(0, members)
    def _(d):
        s = other_member(me, members - 1 - d, members)
        unit = rms_unit(qbuf[own_rows(s, 0)])
        a = dot_nn(unit, updated[0])
        b = dot_nn(unit, updated[1])
        hidden = (a / (1.0 + jnp.exp(-a)) * b).astype(bf16)
        fast_send[s] = (dot_nn(hidden, updated[2]) * gain).astype(bf16)

        @pl.when(s == me)
        def _():
            block_kept(fast_send, fast_recv, fast_r).start()

        @pl.when(s != me)
        def _():
            block_to(fast_send, fast_recv, fast_s, fast_r, s).start()

    @pl.when((parity == 0) & has_upper)
    def _():
        @pl.loop(0, reaching)
        def _(i):
            attend_for_upper(reaching - 1 - i)

    @pl.loop(0, members)
    def _(i):
        attend_and_send(members - 1 - i)

    block_kept(window_send, window_recv, win_r).wait()
    block_kept(fast_send, fast_recv, fast_r).wait()

    @pl.loop(1, members)
    def _(d):
        s = other_member(me, d, members)
        block_to(window_send, window_recv, win_s, win_r, s).wait_recv()
        block_to(fast_send, fast_recv, fast_s, fast_r, s).wait_recv()

    @pl.loop(1, members)
    def _(d):
        s = other_member(me, d, members)
        rates_to(d).wait_send()

        @pl.when((d == 1) | (lax.rem(d, 2) != parity))
        def _():
            for copy in pair_of(d):
                copy.wait_send()

        exchange(q_hbm, qbuf, 0, q_s, q_r, d).wait_send()
        block_to(window_send, window_recv, win_s, win_r, s).wait_send()
        block_to(fast_send, fast_recv, fast_s, fast_r, s).wait_send()

    @pl.loop(0, reaching)
    def _(s):
        @pl.when(has_lower)
        def _():
            query_down(s).wait_send()

        @pl.when(has_upper)
        def _():
            for copy in part_up(s):
                copy.wait_send()

    @pl.loop(0, chunks)
    def _(i):
        inward(i, from_inner, inner_r).wait_send()

        @pl.when(has_outer)
        def _():
            outward(i).wait_send()


def norm_kernel(window_raw, fast_raw, window_ref, fast_ref):
    heads, _, width = window_raw.shape
    for raw, out in ((window_raw, window_ref), (fast_raw, fast_ref)):
        total = 0.0
        for h in range(heads):
            x = raw[h].astype(jnp.float32)
            total = total + jnp.sum(x * x, axis=1, keepdims=True)
        scale = lax.rsqrt(total / (heads * width) + EPSILON)
        for h in range(heads):
            out[:, h * width : (h + 1) * width] = (raw[h].astype(jnp.float32) * scale).astype(
                jnp.bfloat16
            )


def normed_rows(window_raw, fast_raw):
    heads, rows, width = window_raw.shape
    block = 64
    raw = pl.BlockSpec((heads, block, width), lambda i: (0, i, 0))
    done = pl.BlockSpec((block, heads * width), lambda i: (i, 0))
    out = jax.ShapeDtypeStruct((rows, heads * width), jnp.bfloat16)
    return pl.pallas_call(
        norm_kernel,
        grid=(rows // block,),
        out_shape=(out, out),
        in_specs=[raw, raw],
        out_specs=(done, done),
        compiler_params=pltpu.CompilerParams(vmem_limit_bytes=60 * 2**20),
        cost_estimate=pl.CostEstimate(
            flops=8 * rows * heads * width, bytes_accessed=8 * rows * heads * width, transcendentals=0
        ),
    )(window_raw, fast_raw)


def local_kernel(queries, key_rows, value_rows, token_rates, fast_one, fast_three, fast_two, head_gain):
    groups, members = lax.axis_size("grp"), lax.axis_size("mem")
    rows, width = queries.shape[0], fast_one.shape[1]
    pad = -(WINDOW + rows) % 128
    chunk = 128
    chunks = 3 * width // chunk
    bf16, dma = jnp.bfloat16, pltpu.SemaphoreType.DMA
    keys = pltpu.VMEM((pad + WINDOW + members * rows, width), bf16)
    tokens = pltpu.VMEM((members * rows, width), bf16)
    reaching = -(-WINDOW // rows)
    reached = pltpu.VMEM((reaching, rows, width), bf16)
    stats = pltpu.VMEM((reaching, 8, rows), jnp.float32)
    parts = pltpu.VMEM((chunks, chunk, width), bf16)
    blocks = pltpu.VMEM((members, rows, width), bf16)
    matrices = pltpu.VMEM((3, width, width), bf16)
    anywhere = pl.BlockSpec(memory_space=pl.ANY)
    out = jax.ShapeDtypeStruct((members, rows, width), bf16)
    window_raw, fast_raw = pl.pallas_call(
        functools.partial(layer_kernel, (groups, members, rows, width, pad, chunk)),
        out_shape=(out, out),
        in_specs=[anywhere] * 7 + [pl.BlockSpec(memory_space=pltpu.SMEM)],
        out_specs=(anywhere, anywhere),
        scratch_shapes=[
            keys, keys, tokens,
            pltpu.VMEM((members, members, rows), jnp.float32),
            matrices, matrices, pltpu.VMEM((3 * width, width), jnp.float32),
            parts, parts, parts, parts, blocks, blocks,
            tokens, tokens, pltpu.VMEM((members * rows, width), jnp.float32),
            pltpu.VMEM((members * rows, width), jnp.float32),
            reached, reached, reached, stats, stats,
        ]
        + [dma((members,))] * 8
        + [dma((3, members))] * 2
        + [dma((chunks,))] * 4
        + [dma((members,))] * 4
        + [dma((3,))],
        compiler_params=pltpu.CompilerParams(
            collective_id=0, has_side_effects=True, vmem_limit_bytes=56 * 2**20
        ),
        cost_estimate=pl.CostEstimate(
            flops=16 * 2**30, bytes_accessed=10 * 2**20, transcendentals=4 * 2**20
        ),
    )(key_rows, value_rows, queries, token_rates.T, fast_one, fast_three, fast_two, head_gain)
    return normed_rows(window_raw, fast_raw)


def solution(mesh):
    ctx, head = mesh.shape["ctx"], mesh.shape["head"]
    def run(*args):
        members = args[4].shape[0] // head
        split = Mesh(mesh.devices.reshape(ctx // members, members, head), ("grp", "mem", "head"))
        rows = P(("grp", "mem"), "head")
        weights = P("head", None, None)
        groups, width, rows_here = ctx // members, args[4].shape[1], args[0].shape[0] // ctx
        whole_blocks = rows_here % 64 == 0 and width % 128 == 0 and members * rows_here > WINDOW
        pairs = groups % 2 == 0 and members > 1 and members & (members - 1) == 0
        fits = whole_blocks and pairs and members % 8 == 0 and 3 * width // 128 >= members
        return jax.shard_map(
            local_kernel if fits and head == 1 else local,
            mesh=split,
            in_specs=(rows, rows, rows, rows, weights, weights, weights, P("head")),
            out_specs=(rows, rows),
            check_vma=False,
        )(*args)

    return run
```

```python
import functools

import jax
import jax.numpy as jnp
from jax import lax
from jax.experimental import pallas as pl
from jax.experimental.pallas import tpu as pltpu
from jax.sharding import Mesh
from jax.sharding import PartitionSpec as P

WINDOW = 1024
NS_STEPS = 2

COEF_A = 3.4445
COEF_B = -4.775
COEF_C = 2.0315
EPSILON = 1e-06


def rms_heads(block):
    return block / jnp.sqrt(jnp.mean(block * block, axis=-1, keepdims=True) + EPSILON)


def to_heads(rows):
    return lax.all_to_all(rows, "mem", split_axis=1, concat_axis=0, tiled=True)


def to_tokens(rows):
    return lax.all_to_all(rows, "mem", split_axis=0, concat_axis=1, tiled=True)


def with_earlier(rows):
    tokens, groups = rows.shape[0], lax.axis_size("grp")
    parts, missing, distance = [rows], WINDOW, 1
    while missing > 0:
        take = min(missing, tokens)
        pairs = [(i, i + distance) for i in range(groups - distance)]
        parts.insert(0, lax.ppermute(rows[tokens - take :], "grp", pairs))
        missing -= take
        distance += 1
    return jnp.concatenate(parts, axis=0)


def window_attention(q, k, v):
    tokens, width = q.shape
    block = 512 if tokens % 512 == 0 else tokens
    count = tokens // block
    keys, values = with_earlier(k), with_earlier(v)
    reach = WINDOW + block
    keys = jnp.stack([keys[i * block : i * block + reach] for i in range(count)])
    values = jnp.stack([values[i * block : i * block + reach] for i in range(count)])
    scores = jnp.einsum(
        "bqd,bkd->bqk", q.reshape(count, block, width), keys, preferred_element_type=jnp.float32
    ) * width ** (-0.5)
    query_pos = lax.broadcasted_iota(jnp.int32, (count, block, reach), 1) + WINDOW
    key_pos = lax.broadcasted_iota(jnp.int32, (count, block, reach), 2)
    base = lax.broadcasted_iota(jnp.int32, (count, block, reach), 0) * block
    first_key = lax.axis_index("grp") * tokens - WINDOW
    offset = query_pos - key_pos
    allowed = (offset >= 0) & (offset < WINDOW) & (key_pos + base + first_key >= 0)
    scores = jnp.where(allowed, scores, -1e30)
    row_top = jnp.max(scores, axis=-1, keepdims=True)
    exponent = jnp.exp(scores - row_top)
    weights = (exponent / jnp.sum(exponent, axis=-1, keepdims=True)).astype(jnp.bfloat16)
    out = jnp.einsum("bqk,bkd->bqd", weights, values, preferred_element_type=jnp.float32)
    return out.reshape(tokens, width)


def orthogonal(gradient):
    squares = jnp.sum(gradient * gradient)
    current = (gradient / (jnp.sqrt(squares) + 1e-07)).astype(jnp.bfloat16)
    for sweep_index in range(NS_STEPS):
        gram = jnp.einsum(
            "rc,sc->rs", current, current, preferred_element_type=jnp.float32
        ).astype(jnp.bfloat16)
        mixer = (
            COEF_B * gram.astype(jnp.float32)
            + COEF_C * jnp.dot(gram, gram, preferred_element_type=jnp.float32)
        ).astype(jnp.bfloat16)
        current = (
            COEF_A * current.astype(jnp.float32)
            + jnp.dot(mixer, current, preferred_element_type=jnp.float32)
        ).astype(jnp.bfloat16)
    return current


def fast_weights(q, k, v, rates, one, three, two):
    f32 = jnp.float32
    key_normed = rms_heads(k.astype(f32)).astype(jnp.bfloat16)
    query_normed = rms_heads(q.astype(f32)).astype(jnp.bfloat16)
    hidden_one = jnp.dot(key_normed, one, preferred_element_type=f32)
    hidden_three = jnp.dot(key_normed, three, preferred_element_type=f32)
    sigmoid_one = jax.nn.sigmoid(hidden_one)
    active = hidden_one * sigmoid_one
    hidden = (active * hidden_three).astype(jnp.bfloat16)
    delta_out = (-rates * v.astype(f32)).astype(jnp.bfloat16)
    delta_hidden = jnp.einsum("td,fd->tf", delta_out, two, preferred_element_type=f32)
    delta_three = (delta_hidden * active).astype(jnp.bfloat16)
    delta_one = (
        delta_hidden * hidden_three * sigmoid_one * (1.0 + hidden_one * (1.0 - sigmoid_one))
    ).astype(jnp.bfloat16)
    gradient_one = jnp.einsum("td,tf->df", key_normed, delta_one, preferred_element_type=f32)
    gradient_three = jnp.einsum("td,tf->df", key_normed, delta_three, preferred_element_type=f32)
    gradient_two = jnp.einsum("tf,td->fd", hidden, delta_out, preferred_element_type=f32)
    grads = lax.psum(jnp.stack([gradient_one, gradient_three, gradient_two]), "grp")
    new = [
        (old.astype(f32) - orthogonal(grads[i]).astype(f32)).astype(jnp.bfloat16)
        for i, old in enumerate((one, three, two))
    ]
    query_one = jnp.dot(query_normed, new[0], preferred_element_type=f32)
    query_three = jnp.dot(query_normed, new[1], preferred_element_type=f32)
    query_hidden = (jax.nn.silu(query_one) * query_three).astype(jnp.bfloat16)
    return jnp.dot(query_hidden, new[2], preferred_element_type=f32)


def normed(rows):
    rows = rows.astype(jnp.float32)
    heads = lax.axis_size("head")
    total = lax.psum(jnp.sum(rows * rows, axis=1, keepdims=True), "head")
    return (rows / jnp.sqrt(total / (rows.shape[1] * heads) + EPSILON)).astype(jnp.bfloat16)


def local(queries, key_rows, value_rows, token_rates, fast_one, fast_three, fast_two, head_gain):
    me = lax.axis_index("mem")
    k, v, q = to_heads(key_rows), to_heads(value_rows), to_heads(queries)
    first = lax.axis_index("head") * head_gain.shape[0] if token_rates.shape[1] != head_gain.shape[0] else 0
    rates = lax.all_gather(token_rates, "mem", axis=0, tiled=True)
    rates = lax.dynamic_slice_in_dim(rates, me + first, 1, axis=1)
    one, three, two = (
        lax.dynamic_index_in_dim(w, me, 0, keepdims=False) for w in (fast_one, fast_three, fast_two)
    )
    gain = lax.dynamic_index_in_dim(head_gain, me, 0, keepdims=False)
    attended = window_attention(q, k, v)
    fast = fast_weights(q, k, v, rates, one, three, two) * gain
    window_rows = to_tokens(attended.astype(jnp.bfloat16))
    fast_rows = to_tokens(fast.astype(jnp.bfloat16))
    return normed(window_rows), normed(fast_rows)


def dot_nn(a, b):
    return jnp.dot(a, b, preferred_element_type=jnp.float32)


def dot_nt(a, b):
    return lax.dot_general(a, b, (((1,), (1,)), ((), ())), preferred_element_type=jnp.float32)


def dot_tn(a, b):
    return lax.dot_general(a, b, (((0,), (0,)), ((), ())), preferred_element_type=jnp.float32)


def other_member(a, b, count):
    out, bit = 0, 1
    while bit < count:
        out = out + bit * lax.rem(a // bit + b // bit, 2)
        bit *= 2
    return out


def layer_kernel(
    dims, k_hbm, v_hbm, q_hbm, rates_hbm, one_hbm, three_hbm, two_hbm, gain_ref,
    window_recv, fast_recv,
    kbuf, vbuf, qbuf, rbuf, weights, updated, grads, from_outer, from_inner, to_inner, to_outer,
    window_send, fast_send, units, hiddens, gates, slopes,
    k_s, k_r, v_s, v_r, q_s, q_r, r_s, r_r, halo_s, halo_r, outer_r, inner_r, inner_s, outer_s,
    win_s, win_r, fast_s, fast_r, load_sem,
):
    groups, members, rows, width, pad, chunk = dims
    f32, bf16 = jnp.float32, jnp.bfloat16
    me, grp = lax.axis_index("mem"), lax.axis_index("grp")
    base = pad + WINDOW
    reach = base + rows
    stretch = members * rows
    chunks = 3 * width // chunk
    halo_first = (stretch - WINDOW) // rows
    halo_part = (halo_first + 1) * rows - (stretch - WINDOW)
    has_lower, has_upper = grp > 0, grp < groups - 1
    has_outer = jnp.logical_and(has_lower, has_upper)
    in_lower = grp < groups // 2
    inner = jnp.where(in_lower, grp + 1, grp - 1)
    outer = jnp.where(in_lower, grp - 1, grp + 1)
    is_mid = jnp.logical_or(grp == groups // 2 - 1, grp == groups // 2)

    barrier = pltpu.get_barrier_semaphore()
    for d in range(1, members):
        pl.semaphore_signal(barrier, inc=1, device_id={"mem": lax.rem(me + d, members)})

    @pl.when(has_lower)
    def _():
        pl.semaphore_signal(barrier, inc=1, device_id={"grp": grp - 1})

    @pl.when(has_upper)
    def _():
        pl.semaphore_signal(barrier, inc=1, device_id={"grp": grp + 1})

    pl.semaphore_wait(
        barrier, members - 1 + jnp.minimum(grp, 1) + jnp.minimum(groups - 1 - grp, 1)
    )

    def cols(p):
        return pl.ds(pl.multiple_of(p * width, width), width)

    def own_rows(s, first=base):
        return pl.ds(pl.multiple_of(first + s * rows, 16), rows)

    def exchange(hbm, buf, first, send, recv, d):
        peer = other_member(me, d, members)
        return pltpu.make_async_remote_copy(
            src_ref=hbm.at[:, cols(peer)], dst_ref=buf.at[own_rows(me, first)],
            send_sem=send.at[d], recv_sem=recv.at[d], device_id={"mem": peer},
        )

    def kept(hbm, buf, first, recv):
        return pltpu.make_async_copy(
            hbm.at[:, cols(me)], buf.at[own_rows(me, first)], recv.at[0]
        )

    def rates_to(d):
        peer = other_member(me, d, members)
        return pltpu.make_async_remote_copy(
            src_ref=rates_hbm, dst_ref=rbuf.at[me],
            send_sem=r_s.at[d], recv_sem=r_r.at[d], device_id={"mem": peer},
        )

    def block_to(send_buf, recv_buf, send, recv, s):
        d = other_member(me, s, members)
        return pltpu.make_async_remote_copy(
            src_ref=send_buf.at[s], dst_ref=recv_buf.at[me],
            send_sem=send.at[d], recv_sem=recv.at[d], device_id={"mem": s},
        )

    def block_kept(send_buf, recv_buf, recv):
        return pltpu.make_async_copy(send_buf.at[me], recv_buf.at[me], recv.at[0])

    own_rates = pltpu.make_async_copy(rates_hbm, rbuf.at[me], r_r.at[0])
    own_rates.start()
    kept(k_hbm, kbuf, base, k_r).start()
    kept(v_hbm, vbuf, base, v_r).start()
    kept(q_hbm, qbuf, 0, q_r).start()

    parity = lax.rem(me, 2)

    def pair_of(d):
        return (
            exchange(k_hbm, kbuf, base, k_s, k_r, d),
            exchange(v_hbm, vbuf, base, v_s, v_r, d),
        )

    for copy in pair_of(1):
        copy.start()

    @pl.loop(1, members // 2)
    def _(j):
        for copy in pair_of(2 * j + parity):
            copy.start()

    @pl.loop(1, members)
    def _(d):
        rates_to(d).start()

    loads = [
        pltpu.make_async_copy(hbm.at[me], weights.at[i], load_sem.at[i])
        for i, hbm in enumerate((one_hbm, three_hbm, two_hbm))
    ]
    for load in loads:
        load.start()
    kbuf[0:pad] = jnp.zeros((pad, width), bf16)
    vbuf[0:pad] = jnp.zeros((pad, width), bf16)

    @pl.when(grp == 0)
    def _():
        kbuf[pad:base] = jnp.zeros((WINDOW, width), bf16)
        vbuf[pad:base] = jnp.zeros((WINDOW, width), bf16)

    grads[...] = jnp.zeros_like(grads)
    for load in loads:
        load.wait()

    def halo_copy(which, s, size):
        buf = (kbuf, vbuf)[which]
        start = base + s * rows + rows - size
        return pltpu.make_async_remote_copy(
            src_ref=buf.at[pl.ds(pl.multiple_of(start, 16), size)],
            dst_ref=buf.at[pl.ds(pl.multiple_of(start - stretch, 16), size)],
            send_sem=halo_s.at[which, s], recv_sem=halo_r.at[which, s],
            device_id={"grp": grp + 1},
        )

    def for_halo(which, s, present, act):
        @pl.when(jnp.logical_and(present, s == halo_first))
        def _():
            act(halo_copy(which, s, halo_part))

        @pl.when(jnp.logical_and(present, s > halo_first))
        def _():
            act(halo_copy(which, s, rows))

    def queries_to(side):
        @pl.loop(0, members // 2)
        def _(j):
            d = 2 * j + jnp.where(parity == side, 0, 1)

            @pl.when(d > 0)
            def _():
                exchange(q_hbm, qbuf, 0, q_s, q_r, d).start()

    def rms_unit(x):
        x = x.astype(f32)
        return (x * lax.rsqrt(jnp.mean(x * x, axis=1, keepdims=True) + EPSILON)).astype(bf16)

    kept(k_hbm, kbuf, base, k_r).wait()
    kept(v_hbm, vbuf, base, v_r).wait()
    for copy in pair_of(1):
        copy.wait_recv()
    for which in range(2):
        for d in range(2):
            for_halo(which, other_member(me, d, members), has_upper, lambda copy: copy.start())

    @pl.loop(1, members // 2)
    def _(j):
        for copy in pair_of(2 * j + parity):
            copy.wait_send()
        for copy in pair_of(2 * j + 1 - parity):
            copy.start()

    @pl.loop(0, members)
    def _(d):
        @pl.when(d > 1)
        def _():
            exchange(k_hbm, kbuf, base, k_s, k_r, d).wait_recv()

        for_halo(
            0, other_member(me, d, members), jnp.logical_and(has_upper, d > 1),
            lambda copy: copy.start(),
        )
        here = own_rows(other_member(me, d, members))
        there = own_rows(other_member(me, d, members), 0)
        key_unit = rms_unit(kbuf[here])
        a = dot_nn(key_unit, weights[0])
        b = dot_nn(key_unit, weights[1])
        sig = 1.0 / (1.0 + jnp.exp(-a))
        active = a * sig
        units[there] = key_unit
        hiddens[there] = (active * b).astype(bf16)
        gates[there] = active
        slopes[there] = b * sig * (1.0 + a * (1.0 - sig))

    @pl.loop(0, members)
    def _(d):
        s = other_member(me, d, members)
        there = own_rows(s, 0)

        @pl.when(d == 0)
        def _():
            own_rates.wait()

        @pl.when(d > 0)
        def _():
            rates_to(d).wait_recv()

        @pl.when(d > 1)
        def _():
            exchange(v_hbm, vbuf, base, v_s, v_r, d).wait_recv()

        for_halo(1, s, jnp.logical_and(has_upper, d > 1), lambda copy: copy.start())

        @pl.when((d == members // 2) & (parity == 1))
        def _():
            queries_to(0)

        heads_rates = rbuf[s]
        is_mine = lax.broadcasted_iota(jnp.int32, heads_rates.shape, 0) == me
        rate_row = jnp.sum(jnp.where(is_mine, heads_rates, 0.0), axis=0, keepdims=True)
        diagonal = lax.broadcasted_iota(jnp.int32, (rows, rows), 0) == lax.broadcasted_iota(
            jnp.int32, (rows, rows), 1
        )
        rate = jnp.sum(jnp.where(diagonal, rate_row, 0.0), axis=1, keepdims=True)
        delta_out = (-rate * vbuf[own_rows(s)].astype(f32)).astype(bf16)
        dh = dot_nt(delta_out, weights[2])
        key_unit = units[there]
        delta_three = (dh * gates[there]).astype(bf16)
        delta_one = (dh * slopes[there]).astype(bf16)
        grads[0:width] += dot_tn(key_unit, delta_one)
        grads[width : 2 * width] += dot_tn(key_unit, delta_three)
        grads[2 * width : 3 * width] += dot_tn(hiddens[there], delta_out)

    def rows_of(i):
        return pl.ds(pl.multiple_of(i * chunk, chunk), chunk)

    def inward(i, target, recv):
        return pltpu.make_async_remote_copy(
            src_ref=to_inner.at[i], dst_ref=target.at[i],
            send_sem=inner_s.at[i], recv_sem=recv.at[i], device_id={"grp": inner},
        )

    def outward(i):
        return pltpu.make_async_remote_copy(
            src_ref=to_outer.at[i], dst_ref=from_inner.at[i],
            send_sem=outer_s.at[i], recv_sem=inner_r.at[i], device_id={"grp": outer},
        )

    def send_inward(i):
        @pl.when(is_mid)
        def _():
            inward(i, from_inner, inner_r).start()

        @pl.when(jnp.logical_not(is_mid))
        def _():
            inward(i, from_outer, outer_r).start()

    @pl.when(jnp.logical_not(has_outer))
    def _():
        @pl.loop(0, chunks)
        def _(i):
            to_inner[i] = grads[rows_of(i)].astype(bf16)
            send_inward(i)

    def attend(s):
        scores = dot_nt(qbuf[own_rows(s, 0)], kbuf[pl.ds(pl.multiple_of(s * rows, 16), reach)])
        query = lax.broadcasted_iota(jnp.int32, (rows, reach), 0)
        key = lax.broadcasted_iota(jnp.int32, (rows, reach), 1)
        offset = query - key + base
        first = grp * stretch + s * rows - base
        allowed = (offset >= 0) & (offset < WINDOW) & (key + first >= 0)
        scores = jnp.where(allowed, scores, -1e30)
        top = jnp.max(scores, axis=1, keepdims=True)
        exponent = jnp.exp((scores - top) * width ** (-0.5))
        total = jnp.sum(exponent, axis=1, keepdims=True)
        out = dot_nn(
            exponent.astype(bf16), vbuf[pl.ds(pl.multiple_of(s * rows, 16), reach)]
        )
        return (out / total).astype(bf16)

    def orthogonal_update(m):
        gradient = grads[pl.ds(pl.multiple_of(m * width, width), width)]
        squares = jnp.sum(jnp.sum(gradient * gradient, axis=1, keepdims=True), axis=0, keepdims=True)
        current = (gradient / (jnp.sqrt(squares) + 1e-07)).astype(bf16)
        for sweep_index in range(NS_STEPS):
            gram = dot_nt(current, current).astype(bf16)
            mixer = (COEF_B * gram.astype(f32) + COEF_C * dot_nn(gram, gram)).astype(bf16)
            current = (COEF_A * current.astype(f32) + dot_nn(mixer, current)).astype(bf16)
        updated[m] = (weights[m].astype(f32) - current.astype(f32)).astype(bf16)

    def attend_and_send(s):
        piece = s + halo_first
        for which in range(2):
            for_halo(
                which, piece, jnp.logical_and(has_lower, piece < members),
                lambda copy: copy.wait_recv(),
            )
        window_send[s] = attend(s)

        @pl.when(s == me)
        def _():
            block_kept(window_send, window_recv, win_r).start()

        @pl.when(s != me)
        def _():
            block_to(window_send, window_recv, win_s, win_r, s).start()

    per_matrix = width // chunk
    @pl.when(parity == 1)
    def _():
        queries_to(1)

    lag = 2

    @pl.loop(0, chunks + lag)
    def _(i):
        @pl.when(jnp.logical_and(has_outer, i < chunks))
        def _():
            inward(i, from_outer, outer_r).wait_recv()
            partial = grads[rows_of(i)] + from_outer[i].astype(f32)
            to_inner[i] = partial.astype(bf16)
            send_inward(i)

        @pl.when(i >= lag)
        def _():
            j = i - lag
            outward(j).wait_recv()

            @pl.when(is_mid)
            def _():
                grads[rows_of(j)] = to_inner[j].astype(f32) + from_inner[j].astype(f32)

            @pl.when(jnp.logical_not(is_mid))
            def _():
                grads[rows_of(j)] = from_inner[j].astype(f32)

            @pl.when(has_outer)
            def _():
                to_outer[j] = grads[rows_of(j)].astype(bf16)
                outward(j).start()

            @pl.when(lax.rem(j, per_matrix) == per_matrix - 1)
            def _():
                orthogonal_update(j // per_matrix)

        @pl.when((i == chunks - 4) & (parity == 0))
        def _():
            queries_to(0)

        @pl.when((i == chunks) & (parity == 0))
        def _():
            queries_to(1)

    kept(q_hbm, qbuf, 0, q_r).wait()

    @pl.loop(1, members)
    def _(d):
        exchange(q_hbm, qbuf, 0, q_s, q_r, d).wait_recv()

    gain = gain_ref[me]

    @pl.loop(0, members)
    def _(d):
        s = other_member(me, members - 1 - d, members)
        unit = rms_unit(qbuf[own_rows(s, 0)])
        a = dot_nn(unit, updated[0])
        b = dot_nn(unit, updated[1])
        hidden = (a / (1.0 + jnp.exp(-a)) * b).astype(bf16)
        fast_send[s] = (dot_nn(hidden, updated[2]) * gain).astype(bf16)

        @pl.when(s == me)
        def _():
            block_kept(fast_send, fast_recv, fast_r).start()

        @pl.when(s != me)
        def _():
            block_to(fast_send, fast_recv, fast_s, fast_r, s).start()

    @pl.loop(0, members)
    def _(i):
        attend_and_send(members - 1 - i)

    block_kept(window_send, window_recv, win_r).wait()
    block_kept(fast_send, fast_recv, fast_r).wait()

    @pl.loop(1, members)
    def _(d):
        s = other_member(me, d, members)
        block_to(window_send, window_recv, win_s, win_r, s).wait_recv()
        block_to(fast_send, fast_recv, fast_s, fast_r, s).wait_recv()

    @pl.loop(1, members)
    def _(d):
        s = other_member(me, d, members)
        rates_to(d).wait_send()

        @pl.when((d == 1) | (lax.rem(d, 2) != parity))
        def _():
            for copy in pair_of(d):
                copy.wait_send()

        exchange(q_hbm, qbuf, 0, q_s, q_r, d).wait_send()
        block_to(window_send, window_recv, win_s, win_r, s).wait_send()
        block_to(fast_send, fast_recv, fast_s, fast_r, s).wait_send()

    @pl.loop(0, members)
    def _(s):
        for which in range(2):
            for_halo(which, s, has_upper, lambda copy: copy.wait_send())

    @pl.loop(0, chunks)
    def _(i):
        inward(i, from_inner, inner_r).wait_send()

        @pl.when(has_outer)
        def _():
            outward(i).wait_send()


def norm_kernel(window_raw, fast_raw, window_ref, fast_ref):
    heads, _, width = window_raw.shape
    for raw, out in ((window_raw, window_ref), (fast_raw, fast_ref)):
        total = 0.0
        for h in range(heads):
            x = raw[h].astype(jnp.float32)
            total = total + jnp.sum(x * x, axis=1, keepdims=True)
        scale = lax.rsqrt(total / (heads * width) + EPSILON)
        for h in range(heads):
            out[:, h * width : (h + 1) * width] = (raw[h].astype(jnp.float32) * scale).astype(
                jnp.bfloat16
            )


def normed_rows(window_raw, fast_raw):
    heads, rows, width = window_raw.shape
    block = 64
    raw = pl.BlockSpec((heads, block, width), lambda i: (0, i, 0))
    done = pl.BlockSpec((block, heads * width), lambda i: (i, 0))
    out = jax.ShapeDtypeStruct((rows, heads * width), jnp.bfloat16)
    return pl.pallas_call(
        norm_kernel,
        grid=(rows // block,),
        out_shape=(out, out),
        in_specs=[raw, raw],
        out_specs=(done, done),
        compiler_params=pltpu.CompilerParams(vmem_limit_bytes=60 * 2**20),
        cost_estimate=pl.CostEstimate(
            flops=8 * rows * heads * width, bytes_accessed=8 * rows * heads * width, transcendentals=0
        ),
    )(window_raw, fast_raw)


def local_kernel(queries, key_rows, value_rows, token_rates, fast_one, fast_three, fast_two, head_gain):
    groups, members = lax.axis_size("grp"), lax.axis_size("mem")
    rows, width = queries.shape[0], fast_one.shape[1]
    pad = -(WINDOW + rows) % 128
    chunk = 128
    chunks = 3 * width // chunk
    bf16, dma = jnp.bfloat16, pltpu.SemaphoreType.DMA
    keys = pltpu.VMEM((pad + WINDOW + members * rows, width), bf16)
    tokens = pltpu.VMEM((members * rows, width), bf16)
    parts = pltpu.VMEM((chunks, chunk, width), bf16)
    blocks = pltpu.VMEM((members, rows, width), bf16)
    matrices = pltpu.VMEM((3, width, width), bf16)
    anywhere = pl.BlockSpec(memory_space=pl.ANY)
    out = jax.ShapeDtypeStruct((members, rows, width), bf16)
    window_raw, fast_raw = pl.pallas_call(
        functools.partial(layer_kernel, (groups, members, rows, width, pad, chunk)),
        out_shape=(out, out),
        in_specs=[anywhere] * 7 + [pl.BlockSpec(memory_space=pltpu.SMEM)],
        out_specs=(anywhere, anywhere),
        scratch_shapes=[
            keys, keys, tokens,
            pltpu.VMEM((members, members, rows), jnp.float32),
            matrices, matrices, pltpu.VMEM((3 * width, width), jnp.float32),
            parts, parts, parts, parts, blocks, blocks,
            tokens, tokens, pltpu.VMEM((members * rows, width), jnp.float32),
            pltpu.VMEM((members * rows, width), jnp.float32),
        ]
        + [dma((members,))] * 8
        + [dma((2, members))] * 2
        + [dma((chunks,))] * 4
        + [dma((members,))] * 4
        + [dma((3,))],
        compiler_params=pltpu.CompilerParams(
            collective_id=0, has_side_effects=True, vmem_limit_bytes=56 * 2**20
        ),
        cost_estimate=pl.CostEstimate(
            flops=16 * 2**30, bytes_accessed=10 * 2**20, transcendentals=4 * 2**20
        ),
    )(key_rows, value_rows, queries, token_rates.T, fast_one, fast_three, fast_two, head_gain)
    return normed_rows(window_raw, fast_raw)


def solution(mesh):
    ctx, head = mesh.shape["ctx"], mesh.shape["head"]
    def run(*args):
        members = args[4].shape[0] // head
        split = Mesh(mesh.devices.reshape(ctx // members, members, head), ("grp", "mem", "head"))
        rows = P(("grp", "mem"), "head")
        weights = P("head", None, None)
        groups, width, rows_here = ctx // members, args[4].shape[1], args[0].shape[0] // ctx
        whole_blocks = rows_here % 64 == 0 and width % 128 == 0 and members * rows_here > WINDOW
        pairs = groups % 2 == 0 and members > 1 and members & (members - 1) == 0
        fits = whole_blocks and pairs and members % 8 == 0 and 3 * width // 128 >= members
        return jax.shard_map(
            local_kernel if fits and head == 1 else local,
            mesh=split,
            in_specs=(rows, rows, rows, rows, weights, weights, weights, P("head")),
            out_specs=(rows, rows),
            check_vma=False,
        )(*args)

    return run
```
